256 devices in a mesh: slab: 16 (over x_hi, z), face: 4 (over x_lo, core), band: 4 (over y).
Axes of the slice: x: 4 (x_hi: 2, x_lo: 2; x = x_hi * 2 + x_lo), y: 4, z: 8, core: 2. Of those that a mesh axis runs over, the one named last changes fastest.
Arguments:
- wavefunctions: float32 [96, 24, 24, 1024], P('slab', 'face', None, 'band'), may hold values from -6 to 6
- rotation: float32 [1024, 1024], P(None, 'band'), may hold values from -0.1875 to 0.1875
- cell_matrix: float32 [343, 343], replicated, may hold values from -0.02 to 0.02, as said below
- potential: float32 [96, 24, 24], P('slab', 'face'), may hold values from -0.3 to 0.3
- center: float32 [1], replicated, may hold values from -0.2 to 0.2
- halfwidth: float32 [1], replicated, may hold values from 1 to 1.5
Outputs:
- filtered: float32 [96, 24, 24, 1024], P('slab', 'face', None, 'band')
The draws below stay inside these ranges and needn't reach their ends.
Inputs may be any that keep to these rules, and one draw needn't show every extreme that they name: cell_matrix is symmetric.
All inputs are finite; a program needn't handle non-finite values.
Results may differ from the reference program's by a relative error of at most 0.0001.
Values sent between devices are 32-bit elements; how exact they have to be, the bound alone decides.
No kernel may reach another device: no remote copies, remote signals or barrier semaphores. Data moves between devices by JAX's collectives and lax.ppermute only.
A program may use at most 192 MiB of HBM per device.

```python
import math
import jax
import jax.numpy as jnp
from jax import lax

ORDER = 6
BANDS = 1024
DEGREE = 2
NXN = 96
NYN = 24
NZN = 24


def draw_cell_matrix(key, part):
    key = jax.random.fold_in(key, 11)
    node_count = (ORDER + 1) ** 3
    raw = jax.random.uniform(key, (node_count, node_count), jnp.float32, -1.0, 1.0)
    return (raw + raw.T) * 0.01


def block_scale(rng, shape, shards, smallest, top_value):
    loudness, own = 1.0, jax.random.fold_in(rng, 6)
    for dim, shards_of in shards:
        steps = jnp.exp(jax.random.uniform(jax.random.fold_in(own, dim), (shards_of,), jnp.float32, smallest / len(shards), top_value / len(shards)))
        loudness = loudness * jnp.repeat(steps, shape[dim] // shards_of).reshape([-1 if axis == dim else 1 for axis in range(len(shape))])
    return loudness


def bell_draw(rng, extent, width, most, split=(), held_as=jnp.bfloat16):
    result = jax.random.normal(rng, extent, jnp.float32) * width
    if len(split) > 0:
        result = block_scale(rng, extent, split, -0.22, 0.18) * result
    return jnp.clip(result, min=-most, max=most).astype(held_as)


def setup_inputs(seed: int = 0) -> dict:
    keys = jax.random.split(jax.random.key(seed), 7)
    wavefunctions = bell_draw(keys[0], (NXN, NYN, NZN, BANDS), 1.0, 6.0, ((0, 16), (1, 4), (3, 4)), jnp.float32)
    rotation = bell_draw(keys[1], (BANDS, BANDS), BANDS ** -0.5, 0.1875, ((1, 4),), jnp.float32)
    cell_matrix = draw_cell_matrix(jax.random.fold_in(keys[6], 71), 0)
    potential = jnp.clip(jax.random.uniform(keys[3], (NXN, NYN, NZN), jnp.float32, -0.3, 0.3) * block_scale(keys[3], (NXN, NYN, NZN), ((0, 16), (1, 4)), -0.4, 0.0), -0.3, 0.3)
    center = jnp.clip(jax.random.uniform(keys[4], (1,), jnp.float32, -0.2, 0.2), -0.2, 0.2)
    halfwidth = jnp.clip(jax.random.uniform(keys[5], (1,), jnp.float32, 1.0, 1.5), 1.0, 1.5)
    return dict(wavefunctions=wavefunctions, rotation=rotation, cell_matrix=cell_matrix, potential=potential, center=center, halfwidth=halfwidth)


highest = lax.Precision.HIGHEST


def pad_along(values, which_axis, before, behind):
    widths = [(0, 0)] * values.ndim
    widths[which_axis] = (before, behind)
    return jnp.pad(values, widths)


def split_cells(values, which_axis, cell_count):
    regular = lax.slice_in_dim(values, 0, cell_count * ORDER, axis=which_axis)
    regular = regular.reshape(values.shape[:which_axis] + (cell_count, ORDER) + values.shape[which_axis + 1:])
    closing = lax.slice_in_dim(values, ORDER, cell_count * ORDER + 1, stride=ORDER, axis=which_axis)
    closing = jnp.expand_dims(closing, which_axis + 1)
    return jnp.concatenate([regular, closing], which_axis + 1)


def join_cells(values, which_axis):
    cell_count = values.shape[which_axis]
    outer_shape = values.shape[:which_axis]
    inner_shape = values.shape[which_axis + 2:]
    regular = lax.slice_in_dim(values, 0, ORDER, axis=which_axis + 1)
    regular = regular.reshape(outer_shape + (cell_count * ORDER,) + inner_shape)
    closing = lax.slice_in_dim(values, ORDER, ORDER + 1, axis=which_axis + 1)
    spaced = pad_along(closing, which_axis + 1, 0, ORDER - 1)
    spaced = spaced.reshape(outer_shape + (cell_count * ORDER,) + inner_shape)
    spaced = lax.slice_in_dim(spaced, 0, cell_count * ORDER - ORDER + 1, axis=which_axis)
    return pad_along(regular, which_axis, 0, 1) + pad_along(spaced, which_axis, ORDER, 0)


def cell_apply(extended, kernel):
    counts = [(extended.shape[index] - 1) // ORDER for index in range(3)]
    local_cells = split_cells(extended, 0, counts[0])
    local_cells = split_cells(local_cells, 2, counts[1])
    local_cells = split_cells(local_cells, 4, counts[2])
    product = jnp.einsum("ijkpqr,apbqcrn->aibjckn", kernel, local_cells, precision=highest)
    return join_cells(join_cells(join_cells(product, 4), 2), 0)


def fold_end(values, which_axis):
    length = values.shape[which_axis]
    first_slice = lax.slice_in_dim(values, 0, 1, axis=which_axis) + lax.slice_in_dim(values, length - 1, length, axis=which_axis)
    return jnp.concatenate([first_slice, lax.slice_in_dim(values, 1, length - 1, axis=which_axis)], which_axis)


def operate(values, kernel, potential):
    extended = values
    for which_axis in range(3):
        extended = jnp.concatenate([extended, lax.slice_in_dim(extended, 0, 1, axis=which_axis)], which_axis)
    summed = cell_apply(extended, kernel)
    for which_axis in range(3):
        summed = fold_end(summed, which_axis)
    return summed + potential[:, :, :, None] * values


def reference(wavefunctions, rotation, cell_matrix, potential, center, halfwidth):
    node_side = ORDER + 1
    kernel = cell_matrix.reshape((node_side,) * 6)
    band_block = math.gcd(BANDS, 128)
    flattened = wavefunctions.reshape(NXN * NYN * NZN, BANDS)
    columns = rotation.reshape(BANDS, BANDS // band_block, band_block).transpose(1, 0, 2)
    shift_value = center[0]
    scale_value = halfwidth[0]

    def scaled(values):
        return (operate(values, kernel, potential) - shift_value * values) / scale_value

    def filter_block(column_block):
        rotated = jnp.dot(flattened, column_block, precision=highest, preferred_element_type=jnp.float32)
        rotated = rotated.reshape(NXN, NYN, NZN, band_block)
        previous = rotated
        current = scaled(rotated)
        for degree_step in range(DEGREE - 1):
            previous, current = current, 2.0 * scaled(current) - previous
        return current

    blocks = lax.map(filter_block, columns)
    return jnp.moveaxis(blocks, 0, 3).reshape(NXN, NYN, NZN, BANDS)
```

```python
import functools

import jax
import jax.numpy as jnp
import numpy as np
from jax import lax
from jax.experimental import pallas as pl
from jax.experimental.pallas import tpu as pltpu
from jax.sharding import PartitionSpec as P

ORDER = 6
SIDE = ORDER + 1
NZ = 24
LANES = 128
ROWS = 56
OWNED = 36 * NZ
CELL_ROWS = SIDE * ROWS
KPAD = 400
LAYER = NZ * ROWS
XROWS = 3 * ORDER * ROWS + KPAD
F32 = jnp.float32
BF16 = jnp.bfloat16
LIMIT = 48 * 1024 * 1024


def place(x, y):
    if x == 6:
        return y
    if x == 0:
        return 8 + y
    if y == 6:
        return 46 + x - 1
    return 16 + (x - 1) * 6 + y


def selection():
    chosen = np.zeros((KPAD, SIDE**3), np.float32)
    for p in range(SIDE):
        for q in range(SIDE):
            for r in range(SIDE):
                chosen[r * ROWS + place(p, q), (p * SIDE + q) * SIDE + r] = 1.0
    return chosen


def split(values):
    high = values.astype(BF16)
    return high, (values - high.astype(F32)).astype(BF16)


def dot(a, b):
    return jnp.dot(a, b, preferred_element_type=F32)


def prepare_kernel(cell, chosen, chosen_t, rotation, k_high, k_low, r_high, r_low):
    high, low = split(cell[...])
    k_high[...] = dot(dot(chosen[...], high).astype(BF16), chosen_t[...]).astype(BF16)
    k_low[...] = dot(dot(chosen[...], low).astype(BF16), chosen_t[...]).astype(BF16)
    r_high[...], r_low[...] = split(rotation[...])


def cells_product(x_ref, y_ref, xh_ref, xl_ref, k_high, k_low):
    high, low = split(x_ref[...])
    xh_ref[...] = high
    xl_ref[...] = low
    y_ref[...] = jnp.zeros_like(y_ref)
    kh = k_high[...]
    kl = k_low[...]
    step = ORDER * ROWS
    for pair in range(2):
        first, second = 2 * pair * step, (2 * pair + 1) * step
        xh = jnp.concatenate([xh_ref[first : first + KPAD], xh_ref[second : second + KPAD]], 1)
        xl = jnp.concatenate([xl_ref[first : first + KPAD], xl_ref[second : second + KPAD]], 1)
        product = dot(kh, xh) + (dot(kh, xl) + dot(kl, xh))
        y_ref[first : first + CELL_ROWS] += product[:CELL_ROWS, :LANES]
        y_ref[second : second + CELL_ROWS] += product[:CELL_ROWS, LANES:]
    y_ref[0:ROWS] += y_ref[LAYER : LAYER + ROWS]


def first_kernel(w, gx, gy, gxy, k_high, k_low, local, scale, p_out, f0, f6, s0, s6, x_ref, y_ref, xh_ref, xl_ref):
    x_ref[...] = jnp.zeros_like(x_ref)
    for z in range(NZ):
        at = z * ROWS
        x_ref[at : at + 6] = gx[pl.ds(z, 6, stride=NZ)]
        x_ref[at + 6 : at + 7] = gxy[z : z + 1]
        x_ref[at + 8 : at + 14] = w[pl.ds(z, 6, stride=NZ)]
        x_ref[at + 14 : at + 15] = gy[z : z + 1]
        x_ref[at + 16 : at + 46] = w[pl.ds(6 * NZ + z, 30, stride=NZ)]
        x_ref[at + 46 : at + 51] = gy[pl.ds(NZ + z, 5, stride=NZ)]
    x_ref[LAYER : LAYER + ROWS] = x_ref[0:ROWS]
    cells_product(x_ref, y_ref, xh_ref, xl_ref, k_high, k_low)
    p_out[...] = (y_ref[0:LAYER] + local[...] * x_ref[0:LAYER]) * scale[0]
    for z in range(NZ):
        at = z * ROWS
        s6[pl.ds(z, 7, stride=NZ)] = p_out[at : at + 7]
        s0[pl.ds(z, 7, stride=NZ)] = p_out[at + 8 : at + 15]
        f0[z : z + 1] = p_out[at + 8 : at + 9]
        f0[pl.ds(NZ + z, 5, stride=NZ)] = p_out[pl.ds(at + 16, 5, stride=6)]
        f0[6 * NZ + z : 6 * NZ + z + 1] = p_out[at : at + 1]
        f6[z : z + 1] = p_out[at + 14 : at + 15]
        f6[pl.ds(NZ + z, 5, stride=NZ)] = p_out[at + 46 : at + 51]
        f6[6 * NZ + z : 6 * NZ + z + 1] = p_out[at + 6 : at + 7]


def corner_kernel(s0, s6, r0, r6, t0, t6):
    t0[...] = s0[...]
    t6[...] = s6[...]
    t0[0:NZ] += r0[0:NZ]
    t0[6 * NZ : 7 * NZ] += r6[0:NZ]
    t6[0:NZ] += r0[6 * NZ : 7 * NZ]
    t6[6 * NZ : 7 * NZ] += r6[6 * NZ : 7 * NZ]


def second_kernel(p_in, r0, r6, t0, t6, q0, q6, w, k_high, k_low, local, scale, out, push_x, push_y, push_c, x_ref, y_ref, xh_ref, xl_ref, n_ref):
    x_ref[0:LAYER] = p_in[...]
    x_ref[LAYER:] = jnp.zeros((XROWS - LAYER, LANES), F32)
    n_ref[0 : 7 * NZ] = t0[...] + q0[...]
    n_ref[7 * NZ :] = t6[...] + q6[...]
    for z in range(NZ):
        at = z * ROWS
        x_ref[at : at + 7] = n_ref[pl.ds(7 * NZ + z, 7, stride=NZ)]
        x_ref[at + 8 : at + 15] = n_ref[pl.ds(z, 7, stride=NZ)]
        x_ref[pl.ds(at + 16, 5, stride=6)] += r0[pl.ds(NZ + z, 5, stride=NZ)]
        x_ref[at + 46 : at + 51] += r6[pl.ds(NZ + z, 5, stride=NZ)]
    x_ref[LAYER : LAYER + ROWS] = x_ref[0:ROWS]
    cells_product(x_ref, y_ref, xh_ref, xl_ref, k_high, k_low)
    y_ref[0:LAYER] = (y_ref[0:LAYER] + local[...] * x_ref[0:LAYER]) * (2.0 * scale[0])
    for z in range(NZ):
        at = z * ROWS
        out[pl.ds(z, 6, stride=NZ)] = y_ref[at + 8 : at + 14]
        out[pl.ds(6 * NZ + z, 30, stride=NZ)] = y_ref[at + 16 : at + 46]
        push_x[pl.ds(z, 6, stride=NZ)] = y_ref[at : at + 6]
        push_c[z : z + 1] = y_ref[at + 6 : at + 7]
        push_y[z : z + 1] = y_ref[at + 14 : at + 15]
        push_y[pl.ds(NZ + z, 5, stride=NZ)] = y_ref[at + 46 : at + 51]
    out[...] -= w[...]


def finish_kernel(q, rx, ry, rc, out):
    out[...] = q[...]
    out[0 : 6 * NZ] += rx[...]
    for x in range(6):
        out[x * 6 * NZ : x * 6 * NZ + NZ] += ry[x * NZ : (x + 1) * NZ]
    out[0:NZ] += rc[...]


def piece(values, rows, r_high, r_low):
    high, low = split(values)
    rh = r_high[rows]
    return dot(high, rh) + (dot(low, rh) + dot(high, r_low[rows]))


def band_rows(me, steps, chunk):
    owner = lax.rem(me + steps + 4, 4)
    return pl.ds(pl.multiple_of(owner * 256 + chunk * LANES, LANES), LANES)


def near_terms(me, chunk, own, left, right, r_high, r_low):
    return (
        piece(own[...], band_rows(me, 0, chunk), r_high, r_low)
        + piece(left[...], band_rows(me, -1, chunk), r_high, r_low)
        + piece(right[...], band_rows(me, 1, chunk), r_high, r_low)
    )


def far_terms(me, chunk, low_half, high_half, r_high, r_low):
    rows = band_rows(me, 2, chunk)
    return jnp.concatenate(
        [piece(low_half[...], rows, r_high, r_low), piece(high_half[...], rows, r_high, r_low)], 0
    )


def turn_first(me, own, left, right, r_high, r_low, out):
    out[...] = near_terms(me[0], 0, own, left, right, r_high, r_low)


def turn_second(me, total, low_half, high_half, own, left, right, r_high, r_low, out):
    out[...] = total[...] + (
        near_terms(me[0], 1, own, left, right, r_high, r_low)
        + far_terms(me[0], 0, low_half, high_half, r_high, r_low)
    )


def turn_last(me, total, low_half, high_half, r_high, r_low, out):
    out[...] = total[...] + far_terms(me[0], 1, low_half, high_half, r_high, r_low)


VM = pl.BlockSpec(memory_space=pltpu.VMEM)
SM = pl.BlockSpec(memory_space=pltpu.SMEM)


def call(kernel, name, in_specs, shapes, scratch=(), flops=0, moved=0, grid=None, aliases=None):
    return pl.pallas_call(
        kernel,
        name=name,
        in_specs=in_specs,
        out_specs=[VM] * len(shapes),
        out_shape=[jax.ShapeDtypeStruct(*shape) for shape in shapes],
        scratch_shapes=list(scratch),
        compiler_params=pltpu.CompilerParams(vmem_limit_bytes=LIMIT),
        cost_estimate=pl.CostEstimate(flops=flops, bytes_accessed=moved, transcendentals=0),
        input_output_aliases=aliases or {},
    )


OP_SCRATCH = (
    pltpu.VMEM((XROWS, LANES), F32),
    pltpu.VMEM((LAYER + ROWS, LANES), F32),
    pltpu.VMEM((XROWS, LANES), BF16),
    pltpu.VMEM((XROWS, LANES), BF16),
)
OP_FLOPS = 2 * 3 * 512 * 512 * 512


def passed_along(value, axis, steps):
    count = lax.axis_size(axis)
    return lax.ppermute(value, axis, [(s, (s + steps) % count) for s in range(count)])


def passed_diagonal(value, steps):
    slabs, faces = lax.axis_size("slab"), lax.axis_size("face")
    pairs = [
        (a * faces + b, ((a + steps) % slabs) * faces + (b + steps) % faces)
        for a in range(slabs)
        for b in range(faces)
    ]
    return lax.ppermute(value, ("slab", "face"), pairs)


def shards(wavefunctions, rotation, cell_matrix, potential, center, halfwidth):
    chosen = selection()
    me = lax.axis_index("band").astype(jnp.int32).reshape(1)
    scale = 1.0 / halfwidth

    chunks = []
    for j in range(2):
        w = wavefunctions[..., j * LANES : (j + 1) * LANES]
        gx = passed_along(w[0].reshape(6 * NZ, LANES), "slab", -1)
        gy = passed_along(w[:, 0].reshape(6 * NZ, LANES), "face", -1)
        gxy = passed_diagonal(w[0, 0], -1)
        chunks.append((w.reshape(OWNED, LANES), gx, gy, gxy))

    k_high, k_low, r_high, r_low = call(
        prepare_kernel,
        "prepare",
        [VM] * 4,
        [((KPAD, KPAD), BF16)] * 2 + [((1024, 256), BF16)] * 2,
        flops=4 * 2 * KPAD * KPAD * KPAD,
        moved=4 << 20,
    )(cell_matrix, jnp.asarray(chosen, BF16), jnp.asarray(chosen.T, BF16), rotation)

    shifted = potential - center[0]
    by_layer = jnp.transpose(shifted, (2, 0, 1))
    local = jnp.concatenate(
        [
            jnp.zeros((NZ, 8), F32),
            by_layer[:, 0],
            jnp.zeros((NZ, 2), F32),
            by_layer[:, 1:].reshape(NZ, 30),
            jnp.zeros((NZ, 10), F32),
        ],
        1,
    ).reshape(LAYER, 1)

    plane = ((7 * NZ, LANES), F32)
    edge = ((6 * NZ, LANES), F32)
    block = ((OWNED, LANES), F32)

    filtered = []
    for w, gx, gy, gxy in chunks:
        p, f0, f6, s0, s6 = call(
            first_kernel,
            "first",
            [VM] * 7 + [SM],
            [((LAYER, LANES), F32)] + [plane] * 4,
            OP_SCRATCH,
            OP_FLOPS,
            4 << 20,
        )(w, gx, gy, gxy, k_high, k_low, local, scale)
        r0 = passed_along(f6, "face", 1)
        r6 = passed_along(f0, "face", -1)
        t0, t6 = call(corner_kernel, "corner", [VM] * 4, [plane] * 2, moved=1 << 19)(s0, s6, r0, r6)
        q0 = passed_along(t6, "slab", 1)
        q6 = passed_along(t0, "slab", -1)
        q, push_x, push_y, push_c = call(
            second_kernel,
            "second",
            [VM] * 11 + [SM],
            [block, edge, edge, ((NZ, LANES), F32)],
            OP_SCRATCH + (pltpu.VMEM((14 * NZ, LANES), F32),),
            OP_FLOPS,
            4 << 20,
        )(p, r0, r6, t0, t6, q0, q6, w, k_high, k_low, local, scale)
        rx = passed_along(push_x, "slab", 1)
        ry = passed_along(push_y, "face", 1)
        rc = passed_diagonal(push_c, 1)
        (f,) = call(finish_kernel, "finish", [VM] * 4, [block], moved=1 << 20)(q, rx, ry, rc)
        filtered.append(f)

    near, far = [], []
    for f in filtered:
        left = passed_along(f, "band", 1)
        right = passed_along(f, "band", -1)
        near.append((f, left, right))
        far.append(
            (
                passed_along(left[: OWNED // 2], "band", 1),
                passed_along(right[OWNED // 2 :], "band", -1),
            )
        )

    result = [((OWNED, 256), F32)]
    turn_flops = 2 * 3 * 1024 * 256 * 256
    (total,) = call(turn_first, "turn_first", [SM] + [VM] * 5, result, (), 2 * turn_flops, 3 << 20)(
        me, *near[0], r_high, r_low
    )
    (total,) = call(turn_second, "turn_second", [SM] + [VM] * 8, result, (), 3 * turn_flops, 4 << 20, aliases={1: 0})(
        me, total, *far[0], *near[1], r_high, r_low
    )
    (total,) = call(turn_last, "turn_last", [SM] + [VM] * 5, result, (), turn_flops, 3 << 20, aliases={1: 0})(
        me, total, *far[1], r_high, r_low
    )
    return total.reshape(6, 6, NZ, 256)


def solution(mesh):
    placed = (
        P("slab", "face", None, "band"),
        P(None, "band"),
        P(),
        P("slab", "face", None),
        P(),
        P(),
    )
    return jax.shard_map(
        shards,
        mesh=mesh,
        in_specs=placed,
        out_specs=P("slab", "face", None, "band"),
        check_vma=False,
    )
```

```python
import jax
import jax.numpy as jnp
import numpy as np
from jax import lax
from jax.experimental import pallas as pl
from jax.experimental.pallas import tpu as pltpu
from jax.sharding import PartitionSpec as P

ORDER = 6
SIDE = ORDER + 1
NZ = 24
LANES = 128
PARTS = 2
ROWS = 56
CELL_ROWS = SIDE * ROWS
KPAD = 400
LAYER = NZ * ROWS
XROWS = 3 * ORDER * ROWS + KPAD
YROWS = LAYER + ROWS
F32 = jnp.float32
BF16 = jnp.bfloat16
LIMIT = 48 * 1024 * 1024

LINES = (
    [(0, y) for y in range(6)]
    + [(x, 0) for x in range(1, 6)]
    + [(1, 1), (2, 1), (3, 1)]
    + [(4, 1), (5, 1)]
    + [(x, y) for x in range(1, 6) for y in range(2, 6)]
)
LINES1 = 14
LINES2 = 36 - LINES1
SET1 = LINES1 * NZ
SET2 = LINES2 * NZ
EDGE = 6 * NZ
PLANE = 7 * NZ
PLACES = {line: index for index, line in enumerate(LINES)}
PLACES.update({(6, y): 36 + y for y in range(7)})
PLACES.update({(x, 6): 43 + x for x in range(6)})


def selection():
    chosen = np.zeros((KPAD, SIDE**3), np.float32)
    for (p, q), row in PLACES.items():
        for r in range(SIDE):
            chosen[r * ROWS + row, (p * SIDE + q) * SIDE + r] = 1.0
    return chosen


def split(values):
    high = values.astype(BF16)
    return high, (values - high.astype(F32)).astype(BF16)


def dot(a, b):
    return jnp.dot(a, b, preferred_element_type=F32)


def line(index):
    return pl.ds(index * NZ, NZ)


def arrange_kernel(w, w1, w2):
    for index, (x, y) in enumerate(LINES):
        if index < LINES1:
            w1[line(index)] = w[line(x * 6 + y)]
        else:
            w2[line(index - LINES1)] = w[line(x * 6 + y)]


def hold_kernel(w2, left1, out):
    out[...] = w2[...]


def prepare_kernel(me, cell, chosen, chosen_t, rotation, k_high, k_low, r_high, r_low, far_high, far_low):
    high, low = split(cell[...])
    k_high[...] = dot(dot(chosen[...], high).astype(BF16), chosen_t[...]).astype(BF16)
    k_low[...] = dot(dot(chosen[...], low).astype(BF16), chosen_t[...]).astype(BF16)
    for index, steps in enumerate((0, -1, 1, 2)):
        owner = lax.rem(me[0] + steps + 4, 4)
        high, low = split(rotation[pl.ds(pl.multiple_of(owner * 256, 256), 256)])
        if index < 3:
            r_high[pl.ds(index * 256, 256)] = high
            r_low[pl.ds(index * 256, 256)] = low
        else:
            far_high[...] = high
            far_low[...] = low


def turned(values, r_high, r_low):
    high, low = split(values)
    rh = r_high[...]
    return dot(high, rh) + (dot(low, rh) + dot(high, r_low[...]))


def near_kernel(own, left, right, r_high, r_low, total):
    total[...] = turned(jnp.concatenate([own[...], left[...], right[...]], 1), r_high, r_low)


def far_kernel(total, far, far_high, far_low, z1, pull_x):
    values = total[...] + turned(far[...], far_high, far_low)
    for part in range(2):
        lanes = values[:, part * LANES : (part + 1) * LANES]
        z1[pl.ds(part * SET1, SET1)] = lanes
        pull_x[pl.ds(part * EDGE, EDGE)] = lanes[:EDGE]


def edge_kernel(z1, gx, pull_y):
    for part in range(2):
        base = part * PLANE
        pull_y[pl.ds(base, NZ)] = z1[pl.ds(part * SET1, NZ)]
        pull_y[pl.ds(base + NZ, 5 * NZ)] = z1[pl.ds(part * SET1 + EDGE, 5 * NZ)]
        pull_y[pl.ds(base + EDGE, NZ)] = gx[pl.ds(part * EDGE, NZ)]


def cells_product(parts, x_ref, y_ref, xh_ref, xl_ref, k_high, k_low):
    kh = k_high[...]
    kl = k_low[...]
    step = ORDER * ROWS
    for part in range(parts):
        high, low = split(x_ref[part])
        xh_ref[...] = high
        xl_ref[...] = low
        y_ref[part] = jnp.zeros((YROWS, LANES), F32)
        for pair in range(2):
            first, second = 2 * pair * step, (2 * pair + 1) * step
            xh = jnp.concatenate([xh_ref[first : first + KPAD], xh_ref[second : second + KPAD]], 1)
            xl = jnp.concatenate([xl_ref[first : first + KPAD], xl_ref[second : second + KPAD]], 1)
            product = dot(kh, xh) + (dot(kh, xl) + dot(kl, xh))
            y_ref[part, first : first + CELL_ROWS] += product[:CELL_ROWS, :LANES]
            y_ref[part, second : second + CELL_ROWS] += product[:CELL_ROWS, LANES:]
        y_ref[part, 0:ROWS] += y_ref[part, LAYER:YROWS]


def every(start, count):
    return pl.ds(start, count, stride=NZ)


def first_kernel(
    z1, total2, far2, far_high, far_low, gx, gy, k_high, k_low, local, scale,
    z2, p_out, f0, f6, s0, s6, x_ref, y_ref, xh_ref, xl_ref,
):
    values = total2[...] + turned(far2[...], far_high, far_low)
    for part in range(PARTS):
        z2[pl.ds(part * SET2, SET2)] = values[:, part * LANES : (part + 1) * LANES]
    for part in range(PARTS):
        xs = x_ref.at[part]
        xs[LAYER:] = jnp.zeros((XROWS - LAYER, LANES), F32)
        for z in range(NZ):
            at = z * ROWS
            xs[at : at + LINES1] = z1[every(part * SET1 + z, LINES1)]
            xs[at + LINES1 : at + 36] = z2[every(part * SET2 + z, LINES2)]
            xs[at + 36 : at + 42] = gx[every(part * EDGE + z, 6)]
            xs[at + 42 : at + 43] = gy[part * PLANE + EDGE + z : part * PLANE + EDGE + z + 1]
            xs[at + 43 : at + 49] = gy[every(part * PLANE + z, 6)]
            xs[at + 49 : at + 56] = jnp.zeros((7, LANES), F32)
        xs[LAYER:YROWS] = xs[0:ROWS]
    cells_product(PARTS, x_ref, y_ref, xh_ref, xl_ref, k_high, k_low)
    for part in range(PARTS):
        ps = p_out.at[part]
        ps[...] = (y_ref[part, 0:LAYER] + local[...] * x_ref[part, 0:LAYER]) * scale[0]
        base = part * PLANE
        for z in range(NZ):
            at = z * ROWS
            s6[every(base + z, 7)] = ps[at + 36 : at + 43]
            s0[every(base + z, 6)] = ps[at : at + 6]
            s0[base + EDGE + z : base + EDGE + z + 1] = ps[at + 43 : at + 44]
            f0[base + z : base + z + 1] = ps[at : at + 1]
            f0[every(base + NZ + z, 5)] = ps[at + 6 : at + 11]
            f0[base + EDGE + z : base + EDGE + z + 1] = ps[at + 36 : at + 37]
            f6[every(base + z, 6)] = ps[at + 43 : at + 49]
            f6[base + EDGE + z : base + EDGE + z + 1] = ps[at + 42 : at + 43]


def corner_kernel(s0, s6, r0, r6, t0, t6):
    t0[...] = s0[...]
    t6[...] = s6[...]
    for part in range(PARTS):
        low = pl.ds(part * PLANE, NZ)
        high = pl.ds(part * PLANE + EDGE, NZ)
        t0[low] += r0[low]
        t0[high] += r6[low]
        t6[low] += r0[high]
        t6[high] += r6[high]


def second_kernel(
    p_in, r0, r6, t0, t6, q0, q6, v1, v2, k_high, k_low, local, scale,
    out1, out2, push_x, push_y, push_c, x_ref, y_ref, xh_ref, xl_ref, n0, n6,
):
    n0[...] = t0[...] + q0[...]
    n6[...] = t6[...] + q6[...]
    for part in range(PARTS):
        xs = x_ref.at[part]
        xs[0:LAYER] = p_in[part]
        xs[LAYER:] = jnp.zeros((XROWS - LAYER, LANES), F32)
        base = part * PLANE
        for z in range(NZ):
            at = z * ROWS
            xs[at : at + 6] = n0[every(base + z, 6)]
            xs[at + 6 : at + 11] += r0[every(base + NZ + z, 5)]
            xs[at + 36 : at + 43] = n6[every(base + z, 7)]
            xs[at + 43 : at + 44] = n0[base + EDGE + z : base + EDGE + z + 1]
            xs[at + 44 : at + 49] += r6[every(base + NZ + z, 5)]
        xs[LAYER:YROWS] = xs[0:ROWS]
    cells_product(PARTS, x_ref, y_ref, xh_ref, xl_ref, k_high, k_low)
    for part in range(PARTS):
        ys = y_ref.at[part]
        ys[0:LAYER] = (ys[0:LAYER] + local[...] * x_ref[part, 0:LAYER]) * (2.0 * scale[0])
        for z in range(NZ):
            at = z * ROWS
            out1[every(part * SET1 + z, LINES1)] = ys[at : at + LINES1]
            out2[every(part * SET2 + z, LINES2)] = ys[at + LINES1 : at + 36]
            push_x[every(part * EDGE + z, 6)] = ys[at + 36 : at + 42]
            push_c[part * NZ + z : part * NZ + z + 1] = ys[at + 42 : at + 43]
            push_y[every(part * EDGE + z, 6)] = ys[at + 43 : at + 49]
    out1[...] -= v1[...]
    out2[...] -= v2[...]


def last_kernel(q1, q2, rx, ry, rc, out):
    for part in range(PARTS):
        lanes = pl.ds(part * LANES, LANES)
        base = part * EDGE
        for index, (x, y) in enumerate(LINES):
            if index < LINES1:
                value = q1[pl.ds(part * SET1 + index * NZ, NZ)]
                if x == 0:
                    value = value + rx[pl.ds(base + y * NZ, NZ)]
                if y == 0:
                    value = value + ry[pl.ds(base + x * NZ, NZ)]
                if x == 0 and y == 0:
                    value = value + rc[pl.ds(part * NZ, NZ)]
            else:
                value = q2[pl.ds(part * SET2 + (index - LINES1) * NZ, NZ)]
            out[line(x * 6 + y), lanes] = value


VM = pl.BlockSpec(memory_space=pltpu.VMEM)
SM = pl.BlockSpec(memory_space=pltpu.SMEM)


def call(kernel, name, in_specs, shapes, scratch=()):
    inputs, outputs = len(in_specs), len(shapes)

    def body(*refs):
        kernel(*refs[:inputs], *refs[inputs + 1 : inputs + 1 + outputs], *refs[inputs + outputs + 2 :])

    return pl.pallas_call(
        body,
        name=name,
        in_specs=in_specs + [pl.BlockSpec(memory_space=pl.ANY)],
        out_specs=[VM] * outputs + [pl.BlockSpec(memory_space=pl.ANY)],
        out_shape=[jax.ShapeDtypeStruct(*shape) for shape in shapes] + [jax.ShapeDtypeStruct((8, LANES), F32)],
        scratch_shapes=list(scratch),
        compiler_params=pltpu.CompilerParams(vmem_limit_bytes=LIMIT),
        cost_estimate=pl.CostEstimate(flops=1, bytes_accessed=1, transcendentals=0),
        input_output_aliases={inputs: outputs},
    )


class Sequence:
    def __init__(self):
        self.token = jnp.zeros((8, LANES), F32)

    def __call__(self, kernel, *operands):
        *results, self.token = kernel(*operands, self.token)
        return results


def rows_of(count):
    return ((count, LANES), F32)


def passed_along(value, axis, steps):
    count = lax.axis_size(axis)
    return lax.ppermute(value, axis, [(s, (s + steps) % count) for s in range(count)])


def passed_diagonal(value, steps):
    slabs, faces = lax.axis_size("slab"), lax.axis_size("face")
    pairs = [
        (a * faces + b, ((a + steps) % slabs) * faces + (b + steps) % faces)
        for a in range(slabs)
        for b in range(faces)
    ]
    return lax.ppermute(value, ("slab", "face"), pairs)


def local_term(shifted):
    by_layer = jnp.transpose(shifted, (2, 0, 1))
    return jnp.concatenate(
        [
            by_layer[:, 0],
            by_layer[:, 1:, 0],
            by_layer[:, 1:, 1],
            by_layer[:, 1:, 2:].reshape(NZ, 20),
            jnp.zeros((NZ, ROWS - 36), F32),
        ],
        1,
    ).reshape(LAYER, 1)


def shards(wavefunctions, rotation, cell_matrix, potential, center, halfwidth):
    run = Sequence()
    chosen = selection()
    me = lax.axis_index("band").astype(jnp.int32).reshape(1)
    scale = 1.0 / halfwidth
    operator_scratch = [
        pltpu.VMEM((PARTS, XROWS, LANES), F32),
        pltpu.VMEM((PARTS, YROWS, LANES), F32),
        pltpu.VMEM((XROWS, LANES), BF16),
        pltpu.VMEM((XROWS, LANES), BF16),
    ]
    edge, plane = rows_of(PARTS * EDGE), rows_of(PARTS * PLANE)
    wide1, wide2 = ((SET1, 256), F32), ((SET2, 256), F32)
    set1, set2 = rows_of(PARTS * SET1), rows_of(PARTS * SET2)

    w1, w2 = run(call(arrange_kernel, "arrange", [VM], [wide1, wide2]), wavefunctions.reshape(36 * NZ, 256))
    left1 = passed_along(w1, "band", 1)
    right1 = passed_along(w1, "band", -1)
    right2 = passed_along(w2, "band", -1)
    local = local_term(potential - center[0])
    k_high, k_low, r_high, r_low, far_high, far_low = run(
        call(
            prepare_kernel,
            "prepare",
            [SM] + [VM] * 4,
            [((KPAD, KPAD), BF16)] * 2 + [((768, 256), BF16)] * 2 + [((256, 256), BF16)] * 2,
        ),
        me, cell_matrix, jnp.asarray(chosen, BF16), jnp.asarray(chosen.T, BF16), rotation,
    )
    common = (k_high, k_low, local, scale)
    far1 = passed_along(left1, "band", 1)
    (held2,) = run(call(hold_kernel, "hold", [VM, pl.BlockSpec(memory_space=pl.ANY)], [wide2]), w2, left1)
    left2 = passed_along(held2, "band", 1)
    (total1,) = run(call(near_kernel, "near1", [VM] * 5, [wide1]), w1, left1, right1, r_high, r_low)
    z1, pull_x = run(call(far_kernel, "far1", [VM] * 4, [set1, edge]), total1, far1, far_high, far_low)
    gx = passed_along(pull_x, "slab", -1)
    far2 = passed_along(right2, "band", -1)
    (total2,) = run(call(near_kernel, "near2", [VM] * 5, [wide2]), w2, left2, right2, r_high, r_low)
    (pull_y,) = run(call(edge_kernel, "edge", [VM] * 2, [plane]), z1, gx)
    gy = passed_along(pull_y, "face", -1)

    z2, p, f0, f6, s0, s6 = run(
        call(
            first_kernel,
            "first",
            [VM] * 10 + [SM],
            [set2, ((PARTS, LAYER, LANES), F32)] + [plane] * 4,
            operator_scratch,
        ),
        z1, total2, far2, far_high, far_low, gx, gy, *common,
    )
    r0 = passed_along(f6, "face", 1)
    r6 = passed_along(f0, "face", -1)
    t0, t6 = run(call(corner_kernel, "corner", [VM] * 4, [plane] * 2), s0, s6, r0, r6)
    q0 = passed_along(t6, "slab", 1)
    q6 = passed_along(t0, "slab", -1)
    q1, q2, push_x, push_y, push_c = run(
        call(
            second_kernel,
            "second",
            [VM] * 12 + [SM],
            [set1, set2, edge, edge, rows_of(PARTS * NZ)],
            operator_scratch + [pltpu.VMEM((PARTS * PLANE, LANES), F32)] * 2,
        ),
        p, r0, r6, t0, t6, q0, q6, z1, z2, *common,
    )
    rx = passed_along(push_x, "slab", 1)
    ry = passed_along(push_y, "face", 1)
    rc = passed_diagonal(push_c, 1)
    (result,) = run(call(last_kernel, "last", [VM] * 5, [((36 * NZ, 256), F32)]), q1, q2, rx, ry, rc)
    return result.reshape(6, 6, NZ, 256)


def solution(mesh):
    placed = (
        P("slab", "face", None, "band"),
        P(None, "band"),
        P(),
        P("slab", "face", None),
        P(),
        P(),
    )
    return jax.shard_map(
        shards,
        mesh=mesh,
        in_specs=placed,
        out_specs=P("slab", "face", None, "band"),
        check_vma=False,
    )
```

```python
import functools

import jax
import jax.numpy as jnp
import numpy as np
from jax import lax
from jax.experimental import pallas as pl
from jax.experimental.pallas import tpu as pltpu
from jax.sharding import PartitionSpec as P

ORDER = 6
SIDE = ORDER + 1
NZ = 24
LANES = 128
PARTS = 2
ROWS = 56
CELL_ROWS = SIDE * ROWS
KPAD = 400
LAYER = NZ * ROWS
XROWS = 3 * ORDER * ROWS + KPAD
YROWS = LAYER + ROWS
F32 = jnp.float32
BF16 = jnp.bfloat16
LIMIT = 16 * 1024 * 1024
WHOLE = 60 * 1024 * 1024

LINES1 = [(0, y) for y in range(6)] + [(x, 0) for x in range(1, 6)] + [(x, 1) for x in range(1, 4)]
LINES2 = [(x, 1) for x in (4, 5)] + [(x, y) for x in range(1, 6) for y in range(2, 6)]
OWNED = 36 * NZ
SET1 = len(LINES1) * NZ
SET2 = len(LINES2) * NZ
EDGE = 6 * NZ
PLANE = 7 * NZ
PLACES = {(x, y): x * 6 + y for x in range(6) for y in range(6)}
PLACES.update({(6, y): 36 + y for y in range(7)})
PLACES.update({(x, 6): 43 + x for x in range(6)})
CORNERS = ((0, 0), (6, 0), (0, 6), (6, 6))
CROWS = 8
CPAD = 64
CLAYER = NZ * CROWS
CXROWS = 3 * ORDER * CROWS + CPAD


def selection(places, rows, padded):
    chosen = np.zeros((padded, SIDE**3), np.float32)
    for (p, q), row in places:
        for r in range(SIDE):
            chosen[r * rows + row, (p * SIDE + q) * SIDE + r] = 1.0
    return chosen


def split(values):
    high = values.astype(BF16)
    return high, (values - high.astype(F32)).astype(BF16)


def dot(a, b):
    return jnp.dot(a, b, preferred_element_type=F32)


def line(index):
    return pl.ds(index * NZ, NZ)


def carry_out(copies):
    for copy in copies:
        copy.start()
    for copy in copies:
        copy.wait()


def lane_blocks(w, held, sems):
    return [
        pltpu.make_async_copy(
            w.at[:, pl.ds(part * LANES, LANES)], held.at[pl.ds(part * OWNED, OWNED)], sems.at[part]
        )
        for part in range(PARTS)
    ]


def pulls_kernel(w, pull_x, pull_y, pull_c, sems):
    copies = []

    def add(first, rows, out, start, part):
        copies.append(
            pltpu.make_async_copy(
                w.at[pl.ds(first, rows), pl.ds(part * LANES, LANES)],
                out.at[pl.ds(start, rows)],
                sems.at[len(copies)],
            )
        )

    for part in range(PARTS):
        add(0, EDGE, pull_x, part * EDGE, part)
        add(0, NZ, pull_c, part * NZ, part)
        for x in range(6):
            add(x * EDGE, NZ, pull_y, part * EDGE + x * NZ, part)
    carry_out(copies)


def cell_kernel(
    cell, chosen, chosen_t, corners_t, potential, center, halfwidth, k_high, k_low, c_high, c_low, local,
    cell_ref, chosen_ref, chosen_t_ref, corners_t_ref, sems,
):
    pairs = ((cell, cell_ref), (chosen, chosen_ref), (chosen_t, chosen_t_ref), (corners_t, corners_t_ref))
    copies = [pltpu.make_async_copy(source, target, sems.at[index]) for index, (source, target) in enumerate(pairs)]
    for copy in copies:
        copy.start()
    scale = 1.0 / jnp.full((1, LANES), halfwidth[0], F32)
    local[...] = jnp.zeros_like(local)
    for x in range(6):
        shifted = potential[x] - center[0]
        for z in range(NZ):
            local[pl.ds(z * ROWS + x * 6, 6)] = shifted[:, z : z + 1] * scale
    for copy in copies:
        copy.wait()
    for half, k_ref, c_ref in zip(split(cell_ref[...] * scale[:, 0:1]), (k_high, k_low), (c_high, c_low)):
        rows = dot(chosen_ref[...], half).astype(BF16)
        k_ref[...] = dot(rows, chosen_t_ref[...]).astype(BF16)
        c_ref[...] = dot(rows, corners_t_ref[...]).astype(BF16)


def rotation_kernel(me, rotation, r_high, r_low, far_high, far_low):
    for index, steps in enumerate((0, -1, 1, 2)):
        owner = lax.rem(me[0] + steps + 4, 4)
        high, low = split(rotation[pl.ds(pl.multiple_of(owner * 256, 256), 256)])
        if index < 3:
            r_high[pl.ds(index * 256, 256)] = high
            r_low[pl.ds(index * 256, 256)] = low
        else:
            far_high[...] = high
            far_low[...] = low


def turned(values, r_high, r_low):
    high, low = split(values)
    rh = r_high[...]
    return dot(high, rh) + (dot(low, rh) + dot(high, r_low[...]))


def side_by_side(stacked):
    rows = stacked.shape[0] // PARTS
    return [stacked[pl.ds(part * rows, rows)] for part in range(PARTS)]


def near_kernel(own, left, right, r_high, r_low, total):
    pieces = side_by_side(own) + side_by_side(left) + side_by_side(right)
    total[...] = turned(jnp.concatenate(pieces, 1), r_high, r_low)


def line_runs(lines):
    runs = []
    for index, (x, y) in enumerate(lines):
        there = x * 6 + y
        if runs and runs[-1][0] + runs[-1][2] == there:
            runs[-1][2] += 1
        else:
            runs.append([there, index, 1])
    return runs


def write_lines(lines, held, out, sems):
    carry_out(
        [
            pltpu.make_async_copy(
                held.at[pl.ds(here * NZ, count * NZ)], out.at[pl.ds(there * NZ, count * NZ)], sems.at[index]
            )
            for index, (there, here, count) in enumerate(line_runs(lines))
        ]
    )


def relay_kernel(left, right, left_part, right_part):
    rows = left_part.shape[0]
    left_part[...] = left[0:rows]
    right_part[...] = right[rows:]


def far_kernel(lines, total, far_a, far_b, far_high, far_low, *refs):
    out, held, sems = refs[-3:]
    held[...] = total[...] + turned(jnp.concatenate([far_a[...], far_b[...]], 1), far_high, far_low)
    write_lines(lines, held, out, sems)


def fence_kernel(*refs):
    pass


def cells_product(parts, x_ref, y_ref, xh_ref, xl_ref, k_high, k_low):
    kh = k_high[...]
    kl = k_low[...]
    step = ORDER * ROWS
    for part in range(parts):
        high, low = split(x_ref[part])
        xh_ref[...] = high
        xl_ref[...] = low
        y_ref[part] = jnp.zeros((YROWS, LANES), F32)
        for pair in range(2):
            first, second = 2 * pair * step, (2 * pair + 1) * step
            xh = jnp.concatenate([xh_ref[first : first + KPAD], xh_ref[second : second + KPAD]], 1)
            xl = jnp.concatenate([xl_ref[first : first + KPAD], xl_ref[second : second + KPAD]], 1)
            product = dot(kh, xh) + (dot(kh, xl) + dot(kl, xh))
            y_ref[part, first : first + CELL_ROWS] += product[:CELL_ROWS, :LANES]
            y_ref[part, second : second + CELL_ROWS] += product[:CELL_ROWS, LANES:]
        y_ref[part, 0:ROWS] += y_ref[part, LAYER:YROWS]


def every(start, count):
    return pl.ds(start, count, stride=NZ)


def first_kernel(
    w, gx, gy, gc, k_high, k_low, local, p_out, f0, f6, s0, s6, held, x_ref, y_ref, xh_ref, xl_ref, sems
):
    carry_out(lane_blocks(w, held, sems))
    for part in range(PARTS):
        xs = x_ref.at[part]
        xs[LAYER:] = jnp.zeros((XROWS - LAYER, LANES), F32)
        for z in range(NZ):
            at = z * ROWS
            xs[at : at + 36] = held[every(part * OWNED + z, 36)]
            xs[at + 36 : at + 42] = gx[every(part * EDGE + z, 6)]
            xs[at + 42 : at + 43] = gc[part * NZ + z : part * NZ + z + 1]
            xs[at + 43 : at + 49] = gy[every(part * EDGE + z, 6)]
            xs[at + 49 : at + 56] = jnp.zeros((7, LANES), F32)
        xs[LAYER:YROWS] = xs[0:ROWS]
    cells_product(PARTS, x_ref, y_ref, xh_ref, xl_ref, k_high, k_low)
    for part in range(PARTS):
        ps = p_out.at[part]
        ps[...] = y_ref[part, 0:LAYER] + local[...] * x_ref[part, 0:LAYER]
        base = part * PLANE
        for z in range(NZ):
            at = z * ROWS
            s6[every(base + z, 7)] = ps[at + 36 : at + 43]
            s0[every(base + z, 6)] = ps[at : at + 6]
            s0[base + EDGE + z : base + EDGE + z + 1] = ps[at + 43 : at + 44]
            f0[base + z : base + z + 1] = ps[at : at + 1]
            f0[every(base + NZ + z, 5)] = ps[pl.ds(at + 6, 5, stride=6)]
            f0[base + EDGE + z : base + EDGE + z + 1] = ps[at + 36 : at + 37]
            f6[every(base + z, 6)] = ps[at + 43 : at + 49]
            f6[base + EDGE + z : base + EDGE + z + 1] = ps[at + 42 : at + 43]


def cross_kernel(q0, q6, d0, d6):
    for part in range(PARTS):
        base, there = part * PLANE, part * 2 * NZ
        for index, q in enumerate((q0, q6)):
            d0[pl.ds(there + index * NZ, NZ)] = q[pl.ds(base, NZ)]
            d6[pl.ds(there + index * NZ, NZ)] = q[pl.ds(base + EDGE, NZ)]


def second_kernel(p_in, r0, r6, q0, q6, k_high, k_low, local, layers, x_ref, y_ref, xh_ref, xl_ref):
    for part in range(PARTS):
        xs = x_ref.at[part]
        xs[0:LAYER] = p_in[part]
        xs[LAYER:] = jnp.zeros((XROWS - LAYER, LANES), F32)
        base = part * PLANE
        for z in range(NZ):
            at = z * ROWS
            xs[at : at + 6] += q0[every(base + z, 6)]
            xs[at + 36 : at + 43] += q6[every(base + z, 7)]
            xs[at + 43 : at + 44] += q0[base + EDGE + z : base + EDGE + z + 1]
            xs[at : at + 1] += r0[base + z : base + z + 1]
            xs[pl.ds(at + 6, 5, stride=6)] += r0[every(base + NZ + z, 5)]
            xs[at + 36 : at + 37] += r0[base + EDGE + z : base + EDGE + z + 1]
            xs[at + 43 : at + 49] += r6[every(base + z, 6)]
            xs[at + 42 : at + 43] += r6[base + EDGE + z : base + EDGE + z + 1]
        xs[LAYER:YROWS] = xs[0:ROWS]
    cells_product(PARTS, x_ref, y_ref, xh_ref, xl_ref, k_high, k_low)
    for part in range(PARTS):
        layers[part] = 2.0 * (y_ref[part, 0:LAYER] + local[...] * x_ref[part, 0:LAYER])


def third_kernel(
    layers, d0, d6, w, c_high, c_low, local, set1, set2, push_x, push_y, push_c,
    held, c_ref, ch_ref, cl_ref, y_ref, sems,
):
    copies = lane_blocks(w, held, sems)
    for copy in copies:
        copy.start()
    ch, cl = c_high[...], c_low[...]
    step = ORDER * CROWS
    for part in range(PARTS):
        c_ref[...] = jnp.zeros_like(c_ref)
        base = part * 2 * NZ
        for z in range(NZ):
            at = z * CROWS
            c_ref[at : at + 2] = d0[every(base + z, 2)]
            c_ref[at + 2 : at + 4] = d6[every(base + z, 2)]
        c_ref[CLAYER : CLAYER + CROWS] = c_ref[0:CROWS]
        ch_ref[...], cl_ref[...] = split(2.0 * c_ref[...])
        ys = y_ref.at[part]
        ys[0:LAYER] = layers[part]
        ys[LAYER:YROWS] = jnp.zeros((ROWS, LANES), F32)
        for pair in range(2):
            first, second = 2 * pair, 2 * pair + 1
            high = jnp.concatenate([ch_ref[cell * step : cell * step + CPAD] for cell in (first, second)], 1)
            low = jnp.concatenate([cl_ref[cell * step : cell * step + CPAD] for cell in (first, second)], 1)
            product = dot(ch, high) + (dot(ch, low) + dot(cl, high))
            for index, cell in enumerate((first, second)):
                start = cell * ORDER * ROWS
                ys[start : start + CELL_ROWS] += product[:CELL_ROWS, index * LANES : (index + 1) * LANES]
        ys[0:ROWS] += ys[LAYER:YROWS]
        base1, base2 = part * SET1, part * SET2
        for z in range(NZ):
            at = z * ROWS
            ys[at : at + 1] += 2.0 * (local[at : at + 1] * c_ref[z * CROWS : z * CROWS + 1])
            set1[every(base1 + z, 6)] = ys[at : at + 6]
            set1[every(base1 + EDGE + z, 5)] = ys[pl.ds(at + 6, 5, stride=6)]
            set1[every(base1 + 11 * NZ + z, 3)] = ys[pl.ds(at + 7, 3, stride=6)]
            set2[every(base2 + z, 2)] = ys[pl.ds(at + 25, 2, stride=6)]
            for x in range(1, 6):
                set2[every(base2 + (4 * x - 2) * NZ + z, 4)] = ys[at + 6 * x + 2 : at + 6 * x + 6]
            push_x[every(part * EDGE + z, 6)] = ys[at + 36 : at + 42]
            push_c[part * NZ + z : part * NZ + z + 1] = ys[at + 42 : at + 43]
            push_y[every(part * EDGE + z, 6)] = ys[at + 43 : at + 49]
    for copy in copies:
        copy.wait()
    for part in range(PARTS):
        for lines, out in ((LINES1, set1), (LINES2, set2)):
            for index, (x, y) in enumerate(lines):
                out[line(part * len(lines) + index)] -= held[line(part * 36 + x * 6 + y)]


def finish_kernel(set1, rx, ry, rc, out):
    out[...] = set1[...]
    for part in range(PARTS):
        base, edge = part * SET1, part * EDGE
        out[pl.ds(base, EDGE)] += rx[pl.ds(edge, EDGE)]
        out[pl.ds(base, NZ)] += ry[pl.ds(edge, NZ)] + rc[pl.ds(part * NZ, NZ)]
        out[pl.ds(base + EDGE, 5 * NZ)] += ry[pl.ds(edge + NZ, 5 * NZ)]


VM = pl.BlockSpec(memory_space=pltpu.VMEM)
HB = pl.BlockSpec(memory_space=pltpu.HBM)
ANYWHERE = pl.BlockSpec(memory_space=pl.ANY)
SM = pl.BlockSpec(memory_space=pltpu.SMEM)


def call(kernel, name, in_specs, shapes, scratch=(), out=None, aliases=(), flops=10**11, limit=LIMIT, ordered=True):
    inputs, outputs = len(in_specs), len(shapes)
    tokens = 1 if ordered else 0

    def body(*refs):
        kernel(*refs[:inputs], *refs[inputs + tokens : inputs + tokens + outputs], *refs[inputs + outputs + 2 * tokens :])

    if out is None:
        results = [pltpu.VMEM(*shape) for shape in shapes]
    else:
        results = [jax.ShapeDtypeStruct(*shape) for shape in shapes]
    return pl.pallas_call(
        body,
        name=name,
        in_specs=in_specs + [ANYWHERE] * tokens,
        out_specs=[out or VM] * outputs + [ANYWHERE] * tokens,
        out_shape=results + [jax.ShapeDtypeStruct((8, LANES), F32)] * tokens,
        scratch_shapes=list(scratch),
        compiler_params=pltpu.CompilerParams(vmem_limit_bytes=limit),
        cost_estimate=pl.CostEstimate(flops=flops, bytes_accessed=1, transcendentals=0),
        input_output_aliases={**({inputs: outputs} if ordered else {}), **dict(aliases)},
    )


class Sequence:
    def __init__(self):
        self.token = jnp.zeros((8, LANES), F32)

    def __call__(self, kernel, *operands):
        *results, self.token = kernel(*operands, self.token)
        return results


def rows_of(count):
    return ((count, LANES), F32)


def passed_along(value, axis, steps):
    count = lax.axis_size(axis)
    return lax.ppermute(value, axis, [(s, (s + steps) % count) for s in range(count)])


def passed_diagonal(value, steps):
    slabs, faces = lax.axis_size("slab"), lax.axis_size("face")
    pairs = [
        (a * faces + b, ((a + steps) % slabs) * faces + (b + steps) % faces)
        for a in range(slabs)
        for b in range(faces)
    ]
    return lax.ppermute(value, ("slab", "face"), pairs)


def shards(wavefunctions, rotation, cell_matrix, potential, center, halfwidth):
    run = Sequence()
    places = PLACES.items()
    chosen = selection(places, ROWS, KPAD)
    corners_t = selection([(place, row) for row, place in enumerate(CORNERS)], CROWS, CPAD).T
    me = lax.axis_index("band").astype(jnp.int32).reshape(1)
    held = [pltpu.VMEM((PARTS * OWNED, LANES), F32)]
    operator_scratch = [
        pltpu.VMEM((PARTS, XROWS, LANES), F32),
        pltpu.VMEM((PARTS, YROWS, LANES), F32),
        pltpu.VMEM((XROWS, LANES), BF16),
        pltpu.VMEM((XROWS, LANES), BF16),
    ]
    two_copies = [pltpu.SemaphoreType.DMA((PARTS,))]
    edge, plane, corners = rows_of(PARTS * EDGE), rows_of(PARTS * PLANE), rows_of(PARTS * NZ)
    both = rows_of(PARTS * 2 * NZ)
    set1, set2 = rows_of(PARTS * SET1), rows_of(PARTS * SET2)
    wide1, wide2 = ((SET1, 256), F32), ((SET2, 256), F32)
    layer_shape = ((PARTS, LAYER, LANES), F32)
    field = wavefunctions.reshape(OWNED, 256)

    def left(value):
        return passed_along(value, "band", 1)

    def right(value):
        return passed_along(value, "band", -1)

    def fenced(name, *values):
        shapes = [(value.shape, value.dtype) for value in values]
        count = len(values)
        aliases = [(index, index) for index in range(count)]
        return run(call(fence_kernel, name, [ANYWHERE] * count, shapes, out=ANYWHERE, aliases=aliases), *values)

    pull_x, pull_y, pull_c = call(
        pulls_kernel,
        "pulls",
        [HB],
        [edge, edge, corners],
        [pltpu.SemaphoreType.DMA((8 * PARTS,))],
        limit=WHOLE,
        ordered=False,
    )(field)
    gy = passed_along(pull_y, "face", -1)
    gx = passed_along(pull_x, "slab", -1)
    (pull_c,) = fenced("fence_c", pull_c)
    gc = passed_diagonal(pull_c, -1)
    k_high, k_low, c_high, c_low, local = run(
        call(
            cell_kernel,
            "cell",
            [HB] * 4 + [VM] + [SM] * 2,
            [((KPAD, KPAD), BF16)] * 2 + [((KPAD, CPAD), BF16)] * 2 + [((LAYER, LANES), F32)],
            [
                pltpu.VMEM((SIDE**3, SIDE**3), F32),
                pltpu.VMEM((KPAD, SIDE**3), BF16),
                pltpu.VMEM((SIDE**3, KPAD), BF16),
                pltpu.VMEM((SIDE**3, CPAD), BF16),
                pltpu.SemaphoreType.DMA((4,)),
            ],
            flops=1,
        ),
        cell_matrix,
        jnp.asarray(chosen, BF16),
        jnp.asarray(chosen.T, BF16),
        jnp.asarray(corners_t, BF16),
        potential,
        center,
        halfwidth,
    )
    p, f0, f6, s0, s6 = run(
        call(
            first_kernel,
            "first",
            [HB] + [VM] * 6,
            [layer_shape] + [plane] * 4,
            held + operator_scratch + two_copies,
        ),
        field, gx, gy, gc, k_high, k_low, local,
    )
    r0 = passed_along(f6, "face", 1)
    r6 = passed_along(f0, "face", -1)
    q0 = passed_along(s6, "slab", 1)
    q6 = passed_along(s0, "slab", -1)
    r_high, r_low, far_high, far_low = run(
        call(
            rotation_kernel, "rotation", [SM, VM], [((768, 256), BF16)] * 2 + [((256, 256), BF16)] * 2
        ),
        me, rotation,
    )
    e0, e6 = run(call(cross_kernel, "cross", [VM] * 2, [both] * 2), q0, q6)
    d0 = passed_along(e6, "face", 1)
    d6 = passed_along(e0, "face", -1)
    (layers,) = run(
        call(second_kernel, "second", [VM] * 8, [layer_shape], operator_scratch), p, r0, r6, q0, q6, k_high, k_low, local
    )
    v1, v2, push_x, push_y, push_c = run(
        call(
            third_kernel,
            "third",
            [VM] * 3 + [HB] + [VM] * 3,
            [set1, set2, edge, edge, corners],
            held
            + [
                pltpu.VMEM((CXROWS, LANES), F32),
                pltpu.VMEM((CXROWS, LANES), BF16),
                pltpu.VMEM((CXROWS, LANES), BF16),
                pltpu.VMEM((PARTS, YROWS, LANES), F32),
            ]
            + two_copies,
        ),
        layers, d0, d6, field, c_high, c_low, local,
    )
    l2, r2 = left(v2), right(v2)
    push_x, push_y, push_c = fenced("fence_p", push_x, push_y, push_c)
    ry = passed_along(push_y, "face", 1)
    rx = passed_along(push_x, "slab", 1)
    rc = passed_diagonal(push_c, 1)
    (v1,) = run(call(finish_kernel, "finish", [VM] * 4, [set1], flops=1), v1, rx, ry, rc)
    l1, r1 = left(v1), right(v1)


    def relayed(name, from_left, from_right):
        rows = from_left.shape[0] // PARTS
        parts = run(call(relay_kernel, name, [VM] * 2, [rows_of(rows)] * 2), from_left, from_right)
        return left(parts[0]), right(parts[1])

    far2 = relayed("relay2", l2, r2)
    (total2,) = run(call(near_kernel, "near2", [VM] * 5, [wide2]), v2, l2, r2, r_high, r_low)
    far1 = relayed("relay1", l1, r1)
    (total1,) = run(call(near_kernel, "near1", [VM] * 5, [wide1]), v1, l1, r1, r_high, r_low)
    result_shape = [((OWNED, 256), F32)]

    def far_scratch(lines):
        return [pltpu.VMEM((len(lines) * NZ, 256), F32), pltpu.SemaphoreType.DMA((len(line_runs(lines)),))]

    (result,) = run(
        call(functools.partial(far_kernel, LINES2), "far2", [VM] * 5, result_shape, far_scratch(LINES2), out=HB),
        total2, *far2, far_high, far_low,
    )
    (result,) = run(
        call(
            functools.partial(far_kernel, LINES1),
            "last",
            [VM] * 5 + [HB],
            result_shape,
            far_scratch(LINES1),
            out=HB,
            aliases=((5, 0),),
        ),
        total1, *far1, far_high, far_low, result,
    )
    return result.reshape(6, 6, NZ, 256)


def solution(mesh):
    placed = (
        P("slab", "face", None, "band"),
        P(None, "band"),
        P(),
        P("slab", "face", None),
        P(),
        P(),
    )
    return jax.shard_map(
        shards,
        mesh=mesh,
        in_specs=placed,
        out_specs=P("slab", "face", None, "band"),
        check_vma=False,
    )
```

```python
import functools

import jax
import jax.numpy as jnp
import numpy as np
from jax import lax
from jax.experimental import pallas as pl
from jax.experimental.pallas import tpu as pltpu
from jax.sharding import PartitionSpec as P

ORDER = 6
SIDE = ORDER + 1
NZ = 24
LANES = 128
PARTS = 2
ROWS = 56
CELL_ROWS = SIDE * ROWS
KPAD = 400
LAYER = NZ * ROWS
XROWS = 3 * ORDER * ROWS + KPAD
YROWS = LAYER + ROWS
F32 = jnp.float32
BF16 = jnp.bfloat16
LIMIT = 16 * 1024 * 1024
WHOLE = 60 * 1024 * 1024

LINES1 = [(0, y) for y in range(6)] + [(x, 0) for x in range(1, 6)]
LINES2 = [(x, y) for x in range(1, 6) for y in range(1, 6)]
OWNED = 36 * NZ
SET1 = len(LINES1) * NZ
SET2 = len(LINES2) * NZ
EDGE = 6 * NZ
PLANE = 7 * NZ
PLACES = {(x, y): x * 6 + y for x in range(6) for y in range(6)}
PLACES.update({(6, y): 36 + y for y in range(7)})
PLACES.update({(x, 6): 43 + x for x in range(6)})
CORNERS = ((0, 0), (6, 0), (0, 6), (6, 6))
CROWS = 8
CPAD = 64
CLAYER = NZ * CROWS
CXROWS = 3 * ORDER * CROWS + CPAD


def selection(places, rows, padded):
    chosen = np.zeros((padded, SIDE**3), np.float32)
    for (p, q), row in places:
        for r in range(SIDE):
            chosen[r * rows + row, (p * SIDE + q) * SIDE + r] = 1.0
    return chosen


def split(values):
    high = values.astype(BF16)
    return high, (values - high.astype(F32)).astype(BF16)


def dot(a, b):
    return jnp.dot(a, b, preferred_element_type=F32)


def line(index):
    return pl.ds(index * NZ, NZ)


def carry_out(copies):
    for copy in copies:
        copy.start()
    for copy in copies:
        copy.wait()


def lane_blocks(w, held, sems):
    return [
        pltpu.make_async_copy(
            w.at[:, pl.ds(part * LANES, LANES)], held.at[pl.ds(part * OWNED, OWNED)], sems.at[part]
        )
        for part in range(PARTS)
    ]


def pulls_kernel(w, pull_x, pull_y, pull_c, sems):
    copies = []

    def add(first, rows, out, start, part):
        copies.append(
            pltpu.make_async_copy(
                w.at[pl.ds(first, rows), pl.ds(part * LANES, LANES)],
                out.at[pl.ds(start, rows)],
                sems.at[len(copies)],
            )
        )

    for part in range(PARTS):
        add(0, EDGE, pull_x, part * EDGE, part)
        add(0, NZ, pull_c, part * NZ, part)
        for x in range(6):
            add(x * EDGE, NZ, pull_y, part * EDGE + x * NZ, part)
    carry_out(copies)


def cell_kernel(
    cell, chosen, chosen_t, corners_t, potential, center, halfwidth, k_high, k_low, c_high, c_low, local,
    cell_ref, chosen_ref, chosen_t_ref, corners_t_ref, sems,
):
    pairs = ((cell, cell_ref), (chosen, chosen_ref), (chosen_t, chosen_t_ref), (corners_t, corners_t_ref))
    copies = [pltpu.make_async_copy(source, target, sems.at[index]) for index, (source, target) in enumerate(pairs)]
    for copy in copies:
        copy.start()
    scale = 1.0 / jnp.full((1, LANES), halfwidth[0], F32)
    local[...] = jnp.zeros_like(local)
    for x in range(6):
        shifted = potential[x] - center[0]
        for z in range(NZ):
            local[pl.ds(z * ROWS + x * 6, 6)] = shifted[:, z : z + 1] * scale
    for copy in copies:
        copy.wait()
    for half, k_ref, c_ref in zip(split(cell_ref[...] * scale[:, 0:1]), (k_high, k_low), (c_high, c_low)):
        rows = dot(chosen_ref[...], half).astype(BF16)
        k_ref[...] = dot(rows, chosen_t_ref[...]).astype(BF16)
        c_ref[...] = dot(rows, corners_t_ref[...]).astype(BF16)


def rotation_kernel(me, rotation, r_high, r_low, far_high, far_low):
    for index, steps in enumerate((0, -1, 1, 2)):
        owner = lax.rem(me[0] + steps + 4, 4)
        high, low = split(rotation[pl.ds(pl.multiple_of(owner * 256, 256), 256)])
        if index < 3:
            r_high[pl.ds(index * 256, 256)] = high
            r_low[pl.ds(index * 256, 256)] = low
        else:
            far_high[...] = high
            far_low[...] = low


def turned(values, r_high, r_low):
    high, low = split(values)
    rh = r_high[...]
    return dot(high, rh) + (dot(low, rh) + dot(high, r_low[...]))


def side_by_side(stacked):
    rows = stacked.shape[0] // PARTS
    return [stacked[pl.ds(part * rows, rows)] for part in range(PARTS)]


def near_kernel(own, left, right, r_high, r_low, total):
    pieces = side_by_side(own) + side_by_side(left) + side_by_side(right)
    total[...] = turned(jnp.concatenate(pieces, 1), r_high, r_low)


def line_runs(lines):
    runs = []
    for index, (x, y) in enumerate(lines):
        there = x * 6 + y
        if runs and runs[-1][0] + runs[-1][2] == there:
            runs[-1][2] += 1
        else:
            runs.append([there, index, 1])
    return runs


def write_lines(lines, held, out, sems):
    carry_out(
        [
            pltpu.make_async_copy(
                held.at[pl.ds(here * NZ, count * NZ)], out.at[pl.ds(there * NZ, count * NZ)], sems.at[index]
            )
            for index, (there, here, count) in enumerate(line_runs(lines))
        ]
    )


def relay_kernel(left, right, left_part, right_part):
    rows = left_part.shape[0]
    left_part[...] = left[0:rows]
    right_part[...] = right[rows:]


def far_kernel(lines, total, far_a, far_b, far_high, far_low, *refs):
    out, held, sems = refs[-3:]
    held[...] = total[...] + turned(jnp.concatenate([far_a[...], far_b[...]], 1), far_high, far_low)
    write_lines(lines, held, out, sems)


def fence_kernel(*refs):
    pass


def cells_product(parts, x_ref, y_ref, xh_ref, xl_ref, k_high, k_low):
    kh = k_high[...]
    kl = k_low[...]
    step = ORDER * ROWS
    for part in range(parts):
        high, low = split(x_ref[part])
        xh_ref[...] = high
        xl_ref[...] = low
        y_ref[part] = jnp.zeros((YROWS, LANES), F32)
        for pair in range(2):
            first, second = 2 * pair * step, (2 * pair + 1) * step
            xh = jnp.concatenate([xh_ref[first : first + KPAD], xh_ref[second : second + KPAD]], 1)
            xl = jnp.concatenate([xl_ref[first : first + KPAD], xl_ref[second : second + KPAD]], 1)
            product = dot(kh, xh) + (dot(kh, xl) + dot(kl, xh))
            y_ref[part, first : first + CELL_ROWS] += product[:CELL_ROWS, :LANES]
            y_ref[part, second : second + CELL_ROWS] += product[:CELL_ROWS, LANES:]
        y_ref[part, 0:ROWS] += y_ref[part, LAYER:YROWS]


def every(start, count):
    return pl.ds(start, count, stride=NZ)


def first_kernel(
    w, gx, gy, gc, k_high, k_low, local, p_out, f0, f6, s0, s6, held, x_ref, y_ref, xh_ref, xl_ref, sems
):
    carry_out(lane_blocks(w, held, sems))
    for part in range(PARTS):
        xs = x_ref.at[part]
        xs[LAYER:] = jnp.zeros((XROWS - LAYER, LANES), F32)
        for z in range(NZ):
            at = z * ROWS
            xs[at : at + 36] = held[every(part * OWNED + z, 36)]
            xs[at + 36 : at + 42] = gx[every(part * EDGE + z, 6)]
            xs[at + 42 : at + 43] = gc[part * NZ + z : part * NZ + z + 1]
            xs[at + 43 : at + 49] = gy[every(part * EDGE + z, 6)]
            xs[at + 49 : at + 56] = jnp.zeros((7, LANES), F32)
        xs[LAYER:YROWS] = xs[0:ROWS]
    cells_product(PARTS, x_ref, y_ref, xh_ref, xl_ref, k_high, k_low)
    for part in range(PARTS):
        ps = p_out.at[part]
        ps[...] = y_ref[part, 0:LAYER] + local[...] * x_ref[part, 0:LAYER]
        base = part * PLANE
        for z in range(NZ):
            at = z * ROWS
            s6[every(base + z, 7)] = ps[at + 36 : at + 43]
            s0[every(base + z, 6)] = ps[at : at + 6]
            s0[base + EDGE + z : base + EDGE + z + 1] = ps[at + 43 : at + 44]
            f0[base + z : base + z + 1] = ps[at : at + 1]
            f0[every(base + NZ + z, 5)] = ps[pl.ds(at + 6, 5, stride=6)]
            f0[base + EDGE + z : base + EDGE + z + 1] = ps[at + 36 : at + 37]
            f6[every(base + z, 6)] = ps[at + 43 : at + 49]
            f6[base + EDGE + z : base + EDGE + z + 1] = ps[at + 42 : at + 43]


def cross_kernel(q0, q6, d0, d6):
    for part in range(PARTS):
        base, there = part * PLANE, part * 2 * NZ
        for index, q in enumerate((q0, q6)):
            d0[pl.ds(there + index * NZ, NZ)] = q[pl.ds(base, NZ)]
            d6[pl.ds(there + index * NZ, NZ)] = q[pl.ds(base + EDGE, NZ)]


def second_kernel(p_in, r0, r6, q0, q6, k_high, k_low, local, layers, x_ref, y_ref, xh_ref, xl_ref):
    for part in range(PARTS):
        xs = x_ref.at[part]
        xs[0:LAYER] = p_in[part]
        xs[LAYER:] = jnp.zeros((XROWS - LAYER, LANES), F32)
        base = part * PLANE
        for z in range(NZ):
            at = z * ROWS
            xs[at : at + 6] += q0[every(base + z, 6)]
            xs[at + 36 : at + 43] += q6[every(base + z, 7)]
            xs[at + 43 : at + 44] += q0[base + EDGE + z : base + EDGE + z + 1]
            xs[at : at + 1] += r0[base + z : base + z + 1]
            xs[pl.ds(at + 6, 5, stride=6)] += r0[every(base + NZ + z, 5)]
            xs[at + 36 : at + 37] += r0[base + EDGE + z : base + EDGE + z + 1]
            xs[at + 43 : at + 49] += r6[every(base + z, 6)]
            xs[at + 42 : at + 43] += r6[base + EDGE + z : base + EDGE + z + 1]
        xs[LAYER:YROWS] = xs[0:ROWS]
    cells_product(PARTS, x_ref, y_ref, xh_ref, xl_ref, k_high, k_low)
    for part in range(PARTS):
        layers[part] = 2.0 * (y_ref[part, 0:LAYER] + local[...] * x_ref[part, 0:LAYER])


def third_kernel(
    layers, d0, d6, w, c_high, c_low, local, set1, set2, push_x, push_y, push_c,
    held, c_ref, ch_ref, cl_ref, y_ref, sems,
):
    copies = lane_blocks(w, held, sems)
    for copy in copies:
        copy.start()
    ch, cl = c_high[...], c_low[...]
    step = ORDER * CROWS
    for part in range(PARTS):
        c_ref[...] = jnp.zeros_like(c_ref)
        base = part * 2 * NZ
        for z in range(NZ):
            at = z * CROWS
            c_ref[at : at + 2] = d0[every(base + z, 2)]
            c_ref[at + 2 : at + 4] = d6[every(base + z, 2)]
        c_ref[CLAYER : CLAYER + CROWS] = c_ref[0:CROWS]
        ch_ref[...], cl_ref[...] = split(2.0 * c_ref[...])
        ys = y_ref.at[part]
        ys[0:LAYER] = layers[part]
        ys[LAYER:YROWS] = jnp.zeros((ROWS, LANES), F32)
        for pair in range(2):
            first, second = 2 * pair, 2 * pair + 1
            high = jnp.concatenate([ch_ref[cell * step : cell * step + CPAD] for cell in (first, second)], 1)
            low = jnp.concatenate([cl_ref[cell * step : cell * step + CPAD] for cell in (first, second)], 1)
            product = dot(ch, high) + (dot(ch, low) + dot(cl, high))
            for index, cell in enumerate((first, second)):
                start = cell * ORDER * ROWS
                ys[start : start + CELL_ROWS] += product[:CELL_ROWS, index * LANES : (index + 1) * LANES]
        ys[0:ROWS] += ys[LAYER:YROWS]
        base1, base2 = part * SET1, part * SET2
        for z in range(NZ):
            at = z * ROWS
            ys[at : at + 1] += 2.0 * (local[at : at + 1] * c_ref[z * CROWS : z * CROWS + 1])
            set1[every(base1 + z, 6)] = ys[at : at + 6]
            set1[every(base1 + EDGE + z, 5)] = ys[pl.ds(at + 6, 5, stride=6)]
            for x in range(1, 6):
                set2[every(base2 + 5 * (x - 1) * NZ + z, 5)] = ys[at + 6 * x + 1 : at + 6 * x + 6]
            push_x[every(part * EDGE + z, 6)] = ys[at + 36 : at + 42]
            push_c[part * NZ + z : part * NZ + z + 1] = ys[at + 42 : at + 43]
            push_y[every(part * EDGE + z, 6)] = ys[at + 43 : at + 49]
    for copy in copies:
        copy.wait()
    for part in range(PARTS):
        for lines, out in ((LINES1, set1), (LINES2, set2)):
            for index, (x, y) in enumerate(lines):
                out[line(part * len(lines) + index)] -= held[line(part * 36 + x * 6 + y)]


def finish_kernel(set1, rx, ry, rc, out):
    out[...] = set1[...]
    for part in range(PARTS):
        base, edge = part * SET1, part * EDGE
        out[pl.ds(base, EDGE)] += rx[pl.ds(edge, EDGE)]
        out[pl.ds(base, NZ)] += ry[pl.ds(edge, NZ)] + rc[pl.ds(part * NZ, NZ)]
        out[pl.ds(base + EDGE, 5 * NZ)] += ry[pl.ds(edge + NZ, 5 * NZ)]


VM = pl.BlockSpec(memory_space=pltpu.VMEM)
HB = pl.BlockSpec(memory_space=pltpu.HBM)
ANYWHERE = pl.BlockSpec(memory_space=pl.ANY)
SM = pl.BlockSpec(memory_space=pltpu.SMEM)


def call(kernel, name, in_specs, shapes, scratch=(), out=None, aliases=(), flops=10**11, limit=LIMIT, ordered=True):
    inputs, outputs = len(in_specs), len(shapes)
    tokens = 1 if ordered else 0

    def body(*refs):
        kernel(*refs[:inputs], *refs[inputs + tokens : inputs + tokens + outputs], *refs[inputs + outputs + 2 * tokens :])

    if out is None:
        results = [pltpu.VMEM(*shape) for shape in shapes]
    else:
        results = [jax.ShapeDtypeStruct(*shape) for shape in shapes]
    return pl.pallas_call(
        body,
        name=name,
        in_specs=in_specs + [ANYWHERE] * tokens,
        out_specs=[out or VM] * outputs + [ANYWHERE] * tokens,
        out_shape=results + [jax.ShapeDtypeStruct((8, LANES), F32)] * tokens,
        scratch_shapes=list(scratch),
        compiler_params=pltpu.CompilerParams(vmem_limit_bytes=limit),
        cost_estimate=pl.CostEstimate(flops=flops, bytes_accessed=1, transcendentals=0),
        input_output_aliases={**({inputs: outputs} if ordered else {}), **dict(aliases)},
    )


class Sequence:
    def __init__(self):
        self.token = jnp.zeros((8, LANES), F32)

    def __call__(self, kernel, *operands):
        *results, self.token = kernel(*operands, self.token)
        return results


def rows_of(count):
    return ((count, LANES), F32)


def passed_along(value, axis, steps):
    count = lax.axis_size(axis)
    return lax.ppermute(value, axis, [(s, (s + steps) % count) for s in range(count)])


def passed_diagonal(value, steps):
    slabs, faces = lax.axis_size("slab"), lax.axis_size("face")
    pairs = [
        (a * faces + b, ((a + steps) % slabs) * faces + (b + steps) % faces)
        for a in range(slabs)
        for b in range(faces)
    ]
    return lax.ppermute(value, ("slab", "face"), pairs)


def shards(wavefunctions, rotation, cell_matrix, potential, center, halfwidth):
    run = Sequence()
    places = PLACES.items()
    chosen = selection(places, ROWS, KPAD)
    corners_t = selection([(place, row) for row, place in enumerate(CORNERS)], CROWS, CPAD).T
    me = lax.axis_index("band").astype(jnp.int32).reshape(1)
    held = [pltpu.VMEM((PARTS * OWNED, LANES), F32)]
    operator_scratch = [
        pltpu.VMEM((PARTS, XROWS, LANES), F32),
        pltpu.VMEM((PARTS, YROWS, LANES), F32),
        pltpu.VMEM((XROWS, LANES), BF16),
        pltpu.VMEM((XROWS, LANES), BF16),
    ]
    two_copies = [pltpu.SemaphoreType.DMA((PARTS,))]
    edge, plane, corners = rows_of(PARTS * EDGE), rows_of(PARTS * PLANE), rows_of(PARTS * NZ)
    both = rows_of(PARTS * 2 * NZ)
    set1, set2 = rows_of(PARTS * SET1), rows_of(PARTS * SET2)
    wide1, wide2 = ((SET1, 256), F32), ((SET2, 256), F32)
    layer_shape = ((PARTS, LAYER, LANES), F32)
    field = wavefunctions.reshape(OWNED, 256)

    def left(value):
        return passed_along(value, "band", 1)

    def right(value):
        return passed_along(value, "band", -1)

    def fenced(name, *values):
        shapes = [(value.shape, value.dtype) for value in values]
        count = len(values)
        aliases = [(index, index) for index in range(count)]
        return run(call(fence_kernel, name, [ANYWHERE] * count, shapes, out=ANYWHERE, aliases=aliases), *values)

    pull_x, pull_y, pull_c = call(
        pulls_kernel,
        "pulls",
        [HB],
        [edge, edge, corners],
        [pltpu.SemaphoreType.DMA((8 * PARTS,))],
        limit=WHOLE,
        ordered=False,
    )(field)
    gy = passed_along(pull_y, "face", -1)
    gx = passed_along(pull_x, "slab", -1)
    (pull_c,) = fenced("fence_c", pull_c)
    gc = passed_diagonal(pull_c, -1)
    k_high, k_low, c_high, c_low, local = run(
        call(
            cell_kernel,
            "cell",
            [HB] * 4 + [VM] + [SM] * 2,
            [((KPAD, KPAD), BF16)] * 2 + [((KPAD, CPAD), BF16)] * 2 + [((LAYER, LANES), F32)],
            [
                pltpu.VMEM((SIDE**3, SIDE**3), F32),
                pltpu.VMEM((KPAD, SIDE**3), BF16),
                pltpu.VMEM((SIDE**3, KPAD), BF16),
                pltpu.VMEM((SIDE**3, CPAD), BF16),
                pltpu.SemaphoreType.DMA((4,)),
            ],
            flops=1,
        ),
        cell_matrix,
        jnp.asarray(chosen, BF16),
        jnp.asarray(chosen.T, BF16),
        jnp.asarray(corners_t, BF16),
        potential,
        center,
        halfwidth,
    )
    p, f0, f6, s0, s6 = run(
        call(
            first_kernel,
            "first",
            [HB] + [VM] * 6,
            [layer_shape] + [plane] * 4,
            held + operator_scratch + two_copies,
        ),
        field, gx, gy, gc, k_high, k_low, local,
    )
    r0 = passed_along(f6, "face", 1)
    r6 = passed_along(f0, "face", -1)
    q0 = passed_along(s6, "slab", 1)
    q6 = passed_along(s0, "slab", -1)
    r_high, r_low, far_high, far_low = run(
        call(
            rotation_kernel, "rotation", [SM, VM], [((768, 256), BF16)] * 2 + [((256, 256), BF16)] * 2
        ),
        me, rotation,
    )
    e0, e6 = run(call(cross_kernel, "cross", [VM] * 2, [both] * 2), q0, q6)
    d0 = passed_along(e6, "face", 1)
    d6 = passed_along(e0, "face", -1)
    (layers,) = run(
        call(second_kernel, "second", [VM] * 8, [layer_shape], operator_scratch), p, r0, r6, q0, q6, k_high, k_low, local
    )
    v1, v2, push_x, push_y, push_c = run(
        call(
            third_kernel,
            "third",
            [VM] * 3 + [HB] + [VM] * 3,
            [set1, set2, edge, edge, corners],
            held
            + [
                pltpu.VMEM((CXROWS, LANES), F32),
                pltpu.VMEM((CXROWS, LANES), BF16),
                pltpu.VMEM((CXROWS, LANES), BF16),
                pltpu.VMEM((PARTS, YROWS, LANES), F32),
            ]
            + two_copies,
        ),
        layers, d0, d6, field, c_high, c_low, local,
    )
    l2, r2 = left(v2), right(v2)
    push_x, push_y, push_c = fenced("fence_p", push_x, push_y, push_c)
    ry = passed_along(push_y, "face", 1)
    rx = passed_along(push_x, "slab", 1)
    rc = passed_diagonal(push_c, 1)
    (v1,) = run(call(finish_kernel, "finish", [VM] * 4, [set1], flops=1), v1, rx, ry, rc)
    l1, r1 = left(v1), right(v1)


    def relayed(name, from_left, from_right):
        rows = from_left.shape[0] // PARTS
        parts = run(call(relay_kernel, name, [VM] * 2, [rows_of(rows)] * 2), from_left, from_right)
        return left(parts[0]), right(parts[1])

    far2 = relayed("relay2", l2, r2)
    (total2,) = run(call(near_kernel, "near2", [VM] * 5, [wide2]), v2, l2, r2, r_high, r_low)
    far1 = relayed("relay1", l1, r1)
    result_shape = [((OWNED, 256), F32)]

    def far_scratch(lines):
        return [pltpu.VMEM((len(lines) * NZ, 256), F32), pltpu.SemaphoreType.DMA((len(line_runs(lines)),))]

    (result,) = run(
        call(functools.partial(far_kernel, LINES2), "far2", [VM] * 5, result_shape, far_scratch(LINES2), out=HB),
        total2, *far2, far_high, far_low,
    )
    (total1,) = run(call(near_kernel, "near1", [VM] * 5, [wide1]), v1, l1, r1, r_high, r_low)
    (result,) = run(
        call(
            functools.partial(far_kernel, LINES1),
            "last",
            [VM] * 5 + [HB],
            result_shape,
            far_scratch(LINES1),
            out=HB,
            aliases=((5, 0),),
        ),
        total1, *far1, far_high, far_low, result,
    )
    return result.reshape(6, 6, NZ, 256)


def solution(mesh):
    placed = (
        P("slab", "face", None, "band"),
        P(None, "band"),
        P(),
        P("slab", "face", None),
        P(),
        P(),
    )
    return jax.shard_map(
        shards,
        mesh=mesh,
        in_specs=placed,
        out_specs=P("slab", "face", None, "band"),
        check_vma=False,
    )
```

```python
import functools

import jax
import jax.numpy as jnp
import numpy as np
from jax import lax
from jax.experimental import pallas as pl
from jax.experimental.pallas import tpu as pltpu
from jax.sharding import PartitionSpec as P

ORDER = 6
SIDE = ORDER + 1
NZ = 24
LANES = 128
PARTS = 2
ROWS = 56
CELL_ROWS = SIDE * ROWS
KPAD = 400
LAYER = NZ * ROWS
XROWS = 3 * ORDER * ROWS + KPAD
YROWS = LAYER + ROWS
F32 = jnp.float32
BF16 = jnp.bfloat16
LIMIT = 16 * 1024 * 1024
WHOLE = 60 * 1024 * 1024

LINES1 = [(0, y) for y in range(6)] + [(x, 0) for x in range(1, 6)]
LINES2 = [(x, y) for x in range(1, 6) for y in range(1, 6)]
OWNED = 36 * NZ
SET1 = len(LINES1) * NZ
SET2 = len(LINES2) * NZ
EDGE = 6 * NZ
PLANE = 7 * NZ
PLACES = {(x, y): x * 6 + y for x in range(6) for y in range(6)}
PLACES.update({(6, y): 36 + y for y in range(7)})
PLACES.update({(x, 6): 43 + x for x in range(6)})
CORNERS = ((0, 0), (6, 0), (0, 6), (6, 6))
CROWS = 8
CPAD = 64
CLAYER = NZ * CROWS
CXROWS = 3 * ORDER * CROWS + CPAD


def selection(places, rows, padded):
    chosen = np.zeros((padded, SIDE**3), np.float32)
    for (p, q), row in places:
        for r in range(SIDE):
            chosen[r * rows + row, (p * SIDE + q) * SIDE + r] = 1.0
    return chosen


def split(values):
    high = values.astype(BF16)
    return high, (values - high.astype(F32)).astype(BF16)


def dot(a, b):
    return jnp.dot(a, b, preferred_element_type=F32)


def line(index):
    return pl.ds(index * NZ, NZ)


def carry_out(copies):
    for copy in copies:
        copy.start()
    for copy in copies:
        copy.wait()


def lane_blocks(w, held, sems):
    return [
        pltpu.make_async_copy(
            w.at[:, pl.ds(part * LANES, LANES)], held.at[pl.ds(part * OWNED, OWNED)], sems.at[part]
        )
        for part in range(PARTS)
    ]


def pulls_kernel(w, pull_x, pull_y, pull_c, sems):
    copies = []

    def add(first, rows, out, start, part):
        copies.append(
            pltpu.make_async_copy(
                w.at[pl.ds(first, rows), pl.ds(part * LANES, LANES)],
                out.at[pl.ds(start, rows)],
                sems.at[len(copies)],
            )
        )

    for part in range(PARTS):
        add(0, EDGE, pull_x, part * EDGE, part)
        add(0, NZ, pull_c, part * NZ, part)
        for x in range(6):
            add(x * EDGE, NZ, pull_y, part * EDGE + x * NZ, part)
    carry_out(copies)


def cell_kernel(
    cell, chosen, chosen_t, corners_t, potential, center, halfwidth, k_high, k_low, c_high, c_low, local,
    cell_ref, chosen_ref, chosen_t_ref, corners_t_ref, sems,
):
    pairs = ((cell, cell_ref), (chosen, chosen_ref), (chosen_t, chosen_t_ref), (corners_t, corners_t_ref))
    copies = [pltpu.make_async_copy(source, target, sems.at[index]) for index, (source, target) in enumerate(pairs)]
    for copy in copies:
        copy.start()
    scale = 1.0 / jnp.full((1, LANES), halfwidth[0], F32)
    local[...] = jnp.zeros_like(local)
    for x in range(6):
        shifted = potential[x] - center[0]
        for z in range(NZ):
            local[pl.ds(z * ROWS + x * 6, 6)] = shifted[:, z : z + 1] * scale
    for copy in copies:
        copy.wait()
    for half, k_ref, c_ref in zip(split(cell_ref[...] * scale[:, 0:1]), (k_high, k_low), (c_high, c_low)):
        rows = dot(chosen_ref[...], half).astype(BF16)
        k_ref[...] = dot(rows, chosen_t_ref[...]).astype(BF16)
        c_ref[...] = dot(rows, corners_t_ref[...]).astype(BF16)


def rotation_kernel(me, rotation, r_high, r_low, far_high, far_low):
    for index, steps in enumerate((0, -1, 1, 2)):
        owner = lax.rem(me[0] + steps + 4, 4)
        high, low = split(rotation[pl.ds(pl.multiple_of(owner * 256, 256), 256)])
        if index < 3:
            r_high[pl.ds(index * 256, 256)] = high
            r_low[pl.ds(index * 256, 256)] = low
        else:
            far_high[...] = high
            far_low[...] = low


def turned(values, r_high, r_low):
    high, low = split(values)
    rh = r_high[...]
    return dot(high, rh) + (dot(low, rh) + dot(high, r_low[...]))


def side_by_side(stacked):
    rows = stacked.shape[0] // PARTS
    return [stacked[pl.ds(part * rows, rows)] for part in range(PARTS)]


def near_kernel(own, left, right, r_high, r_low, total):
    pieces = side_by_side(own) + side_by_side(left) + side_by_side(right)
    total[...] = turned(jnp.concatenate(pieces, 1), r_high, r_low)


def line_runs(lines):
    runs = []
    for index, (x, y) in enumerate(lines):
        there = x * 6 + y
        if runs and runs[-1][0] + runs[-1][2] == there:
            runs[-1][2] += 1
        else:
            runs.append([there, index, 1])
    return runs


def write_lines(lines, held, out, sems):
    carry_out(
        [
            pltpu.make_async_copy(
                held.at[pl.ds(here * NZ, count * NZ)], out.at[pl.ds(there * NZ, count * NZ)], sems.at[index]
            )
            for index, (there, here, count) in enumerate(line_runs(lines))
        ]
    )


def relay_kernel(left, right, left_part, right_part):
    rows = left_part.shape[0]
    left_part[...] = left[0:rows]
    right_part[...] = right[rows:]


def far_kernel(lines, total, far_a, far_b, far_high, far_low, *refs):
    out, held, sems = refs[-3:]
    held[...] = total[...] + turned(jnp.concatenate([far_a[...], far_b[...]], 1), far_high, far_low)
    write_lines(lines, held, out, sems)


def fence_kernel(*refs):
    pass


def cells_product(parts, x_ref, y_ref, xh_ref, xl_ref, k_high, k_low):
    kh = k_high[...]
    kl = k_low[...]
    step = ORDER * ROWS
    for part in range(parts):
        high, low = split(x_ref[part])
        xh_ref[...] = high
        xl_ref[...] = low
        y_ref[part] = jnp.zeros((YROWS, LANES), F32)
        for pair in range(2):
            first, second = 2 * pair * step, (2 * pair + 1) * step
            xh = jnp.concatenate([xh_ref[first : first + KPAD], xh_ref[second : second + KPAD]], 1)
            xl = jnp.concatenate([xl_ref[first : first + KPAD], xl_ref[second : second + KPAD]], 1)
            product = dot(kh, xh) + (dot(kh, xl) + dot(kl, xh))
            y_ref[part, first : first + CELL_ROWS] += product[:CELL_ROWS, :LANES]
            y_ref[part, second : second + CELL_ROWS] += product[:CELL_ROWS, LANES:]
        y_ref[part, 0:ROWS] += y_ref[part, LAYER:YROWS]


def every(start, count):
    return pl.ds(start, count, stride=NZ)


def first_kernel(
    w, gx, gy, gc, k_high, k_low, local, p_out, f0, f6, s0, s6, held, x_ref, y_ref, xh_ref, xl_ref, sems
):
    carry_out(lane_blocks(w, held, sems))
    for part in range(PARTS):
        xs = x_ref.at[part]
        xs[LAYER:] = jnp.zeros((XROWS - LAYER, LANES), F32)
        for z in range(NZ):
            at = z * ROWS
            xs[at : at + 36] = held[every(part * OWNED + z, 36)]
            xs[at + 36 : at + 42] = gx[every(part * EDGE + z, 6)]
            xs[at + 42 : at + 43] = gc[part * NZ + z : part * NZ + z + 1]
            xs[at + 43 : at + 49] = gy[every(part * EDGE + z, 6)]
            xs[at + 49 : at + 56] = jnp.zeros((7, LANES), F32)
        xs[LAYER:YROWS] = xs[0:ROWS]
    cells_product(PARTS, x_ref, y_ref, xh_ref, xl_ref, k_high, k_low)
    for part in range(PARTS):
        ps = p_out.at[part]
        ps[...] = y_ref[part, 0:LAYER] + local[...] * x_ref[part, 0:LAYER]
        base = part * PLANE
        for z in range(NZ):
            at = z * ROWS
            s6[every(base + z, 7)] = ps[at + 36 : at + 43]
            s0[every(base + z, 6)] = ps[at : at + 6]
            s0[base + EDGE + z : base + EDGE + z + 1] = ps[at + 43 : at + 44]
            f0[base + z : base + z + 1] = ps[at : at + 1]
            f0[every(base + NZ + z, 5)] = ps[pl.ds(at + 6, 5, stride=6)]
            f0[base + EDGE + z : base + EDGE + z + 1] = ps[at + 36 : at + 37]
            f6[every(base + z, 6)] = ps[at + 43 : at + 49]
            f6[base + EDGE + z : base + EDGE + z + 1] = ps[at + 42 : at + 43]


def cross_kernel(q0, q6, d0, d6):
    for part in range(PARTS):
        base, there = part * PLANE, part * 2 * NZ
        for index, q in enumerate((q0, q6)):
            d0[pl.ds(there + index * NZ, NZ)] = q[pl.ds(base, NZ)]
            d6[pl.ds(there + index * NZ, NZ)] = q[pl.ds(base + EDGE, NZ)]


def second_kernel(p_in, r0, r6, q0, q6, k_high, k_low, local, layers, x_ref, y_ref, xh_ref, xl_ref):
    for part in range(PARTS):
        xs = x_ref.at[part]
        xs[0:LAYER] = p_in[part]
        xs[LAYER:] = jnp.zeros((XROWS - LAYER, LANES), F32)
        base = part * PLANE
        for z in range(NZ):
            at = z * ROWS
            xs[at : at + 6] += q0[every(base + z, 6)]
            xs[at + 36 : at + 43] += q6[every(base + z, 7)]
            xs[at + 43 : at + 44] += q0[base + EDGE + z : base + EDGE + z + 1]
            xs[at : at + 1] += r0[base + z : base + z + 1]
            xs[pl.ds(at + 6, 5, stride=6)] += r0[every(base + NZ + z, 5)]
            xs[at + 36 : at + 37] += r0[base + EDGE + z : base + EDGE + z + 1]
            xs[at + 43 : at + 49] += r6[every(base + z, 6)]
            xs[at + 42 : at + 43] += r6[base + EDGE + z : base + EDGE + z + 1]
        xs[LAYER:YROWS] = xs[0:ROWS]
    cells_product(PARTS, x_ref, y_ref, xh_ref, xl_ref, k_high, k_low)
    for part in range(PARTS):
        layers[part] = 2.0 * (y_ref[part, 0:LAYER] + local[...] * x_ref[part, 0:LAYER])


def third_kernel(
    layers, d0, d6, w, c_high, c_low, local, set1, set2, push_x, push_y, push_c,
    held, c_ref, ch_ref, cl_ref, y_ref, sems,
):
    copies = lane_blocks(w, held, sems)
    for copy in copies:
        copy.start()
    ch, cl = c_high[...], c_low[...]
    step = ORDER * CROWS
    for part in range(PARTS):
        c_ref[...] = jnp.zeros_like(c_ref)
        base = part * 2 * NZ
        for z in range(NZ):
            at = z * CROWS
            c_ref[at : at + 2] = d0[every(base + z, 2)]
            c_ref[at + 2 : at + 4] = d6[every(base + z, 2)]
        c_ref[CLAYER : CLAYER + CROWS] = c_ref[0:CROWS]
        ch_ref[...], cl_ref[...] = split(2.0 * c_ref[...])
        ys = y_ref.at[part]
        ys[0:LAYER] = layers[part]
        ys[LAYER:YROWS] = jnp.zeros((ROWS, LANES), F32)
        for pair in range(2):
            first, second = 2 * pair, 2 * pair + 1
            high = jnp.concatenate([ch_ref[cell * step : cell * step + CPAD] for cell in (first, second)], 1)
            low = jnp.concatenate([cl_ref[cell * step : cell * step + CPAD] for cell in (first, second)], 1)
            product = dot(ch, high) + (dot(ch, low) + dot(cl, high))
            for index, cell in enumerate((first, second)):
                start = cell * ORDER * ROWS
                ys[start : start + CELL_ROWS] += product[:CELL_ROWS, index * LANES : (index + 1) * LANES]
        ys[0:ROWS] += ys[LAYER:YROWS]
        base1, base2 = part * SET1, part * SET2
        for z in range(NZ):
            at = z * ROWS
            ys[at : at + 1] += 2.0 * (local[at : at + 1] * c_ref[z * CROWS : z * CROWS + 1])
            set1[every(base1 + z, 6)] = ys[at : at + 6]
            set1[every(base1 + EDGE + z, 5)] = ys[pl.ds(at + 6, 5, stride=6)]
            for x in range(1, 6):
                set2[every(base2 + 5 * (x - 1) * NZ + z, 5)] = ys[at + 6 * x + 1 : at + 6 * x + 6]
            push_x[every(part * EDGE + z, 6)] = ys[at + 36 : at + 42]
            push_c[part * NZ + z : part * NZ + z + 1] = ys[at + 42 : at + 43]
            push_y[every(part * EDGE + z, 6)] = ys[at + 43 : at + 49]
    for copy in copies:
        copy.wait()
    for part in range(PARTS):
        for lines, out in ((LINES1, set1), (LINES2, set2)):
            for index, (x, y) in enumerate(lines):
                out[line(part * len(lines) + index)] -= held[line(part * 36 + x * 6 + y)]


def finish_kernel(set1, rx, ry, rc, out):
    out[...] = set1[...]
    for part in range(PARTS):
        base, edge = part * SET1, part * EDGE
        out[pl.ds(base, EDGE)] += rx[pl.ds(edge, EDGE)]
        out[pl.ds(base, NZ)] += ry[pl.ds(edge, NZ)] + rc[pl.ds(part * NZ, NZ)]
        out[pl.ds(base + EDGE, 5 * NZ)] += ry[pl.ds(edge + NZ, 5 * NZ)]


VM = pl.BlockSpec(memory_space=pltpu.VMEM)
HB = pl.BlockSpec(memory_space=pltpu.HBM)
ANYWHERE = pl.BlockSpec(memory_space=pl.ANY)
SM = pl.BlockSpec(memory_space=pltpu.SMEM)


def call(kernel, name, in_specs, shapes, scratch=(), out=None, aliases=(), flops=10**10, limit=LIMIT, ordered=True):
    inputs, outputs = len(in_specs), len(shapes)
    tokens = 1 if ordered else 0

    def body(*refs):
        kernel(*refs[:inputs], *refs[inputs + tokens : inputs + tokens + outputs], *refs[inputs + outputs + 2 * tokens :])

    if out is None:
        results = [pltpu.VMEM(*shape) for shape in shapes]
    else:
        results = [jax.ShapeDtypeStruct(*shape) for shape in shapes]
    return pl.pallas_call(
        body,
        name=name,
        in_specs=in_specs + [ANYWHERE] * tokens,
        out_specs=[out or VM] * outputs + [ANYWHERE] * tokens,
        out_shape=results + [jax.ShapeDtypeStruct((8, LANES), F32)] * tokens,
        scratch_shapes=list(scratch),
        compiler_params=pltpu.CompilerParams(vmem_limit_bytes=limit),
        cost_estimate=pl.CostEstimate(flops=flops, bytes_accessed=1, transcendentals=0),
        input_output_aliases={**({inputs: outputs} if ordered else {}), **dict(aliases)},
    )


class Sequence:
    def __init__(self):
        self.token = jnp.zeros((8, LANES), F32)

    def __call__(self, kernel, *operands):
        *results, self.token = kernel(*operands, self.token)
        return results


def rows_of(count):
    return ((count, LANES), F32)


def passed_along(value, axis, steps):
    count = lax.axis_size(axis)
    return lax.ppermute(value, axis, [(s, (s + steps) % count) for s in range(count)])


def passed_diagonal(value, steps):
    slabs, faces = lax.axis_size("slab"), lax.axis_size("face")
    pairs = [
        (a * faces + b, ((a + steps) % slabs) * faces + (b + steps) % faces)
        for a in range(slabs)
        for b in range(faces)
    ]
    return lax.ppermute(value, ("slab", "face"), pairs)


def shards(wavefunctions, rotation, cell_matrix, potential, center, halfwidth):
    run = Sequence()
    places = PLACES.items()
    chosen = selection(places, ROWS, KPAD)
    corners_t = selection([(place, row) for row, place in enumerate(CORNERS)], CROWS, CPAD).T
    me = lax.axis_index("band").astype(jnp.int32).reshape(1)
    held = [pltpu.VMEM((PARTS * OWNED, LANES), F32)]
    operator_scratch = [
        pltpu.VMEM((PARTS, XROWS, LANES), F32),
        pltpu.VMEM((PARTS, YROWS, LANES), F32),
        pltpu.VMEM((XROWS, LANES), BF16),
        pltpu.VMEM((XROWS, LANES), BF16),
    ]
    two_copies = [pltpu.SemaphoreType.DMA((PARTS,))]
    edge, plane, corners = rows_of(PARTS * EDGE), rows_of(PARTS * PLANE), rows_of(PARTS * NZ)
    both = rows_of(PARTS * 2 * NZ)
    set1, set2 = rows_of(PARTS * SET1), rows_of(PARTS * SET2)
    wide1, wide2 = ((SET1, 256), F32), ((SET2, 256), F32)
    layer_shape = ((PARTS, LAYER, LANES), F32)
    field = wavefunctions.reshape(OWNED, 256)

    def left(value):
        return passed_along(value, "band", 1)

    def right(value):
        return passed_along(value, "band", -1)

    def fenced(name, *values):
        shapes = [(value.shape, value.dtype) for value in values]
        count = len(values)
        aliases = [(index, index) for index in range(count)]
        return run(call(fence_kernel, name, [ANYWHERE] * count, shapes, out=ANYWHERE, aliases=aliases), *values)

    pull_x, pull_y, pull_c = call(
        pulls_kernel,
        "pulls",
        [HB],
        [edge, edge, corners],
        [pltpu.SemaphoreType.DMA((8 * PARTS,))],
        limit=WHOLE,
        ordered=False,
    )(field)
    gy = passed_along(pull_y, "face", -1)
    gx = passed_along(pull_x, "slab", -1)
    (pull_c,) = fenced("fence_c", pull_c)
    gc = passed_diagonal(pull_c, -1)
    k_high, k_low, c_high, c_low, local = run(
        call(
            cell_kernel,
            "cell",
            [HB] * 4 + [VM] + [SM] * 2,
            [((KPAD, KPAD), BF16)] * 2 + [((KPAD, CPAD), BF16)] * 2 + [((LAYER, LANES), F32)],
            [
                pltpu.VMEM((SIDE**3, SIDE**3), F32),
                pltpu.VMEM((KPAD, SIDE**3), BF16),
                pltpu.VMEM((SIDE**3, KPAD), BF16),
                pltpu.VMEM((SIDE**3, CPAD), BF16),
                pltpu.SemaphoreType.DMA((4,)),
            ],
            flops=1,
        ),
        cell_matrix,
        jnp.asarray(chosen, BF16),
        jnp.asarray(chosen.T, BF16),
        jnp.asarray(corners_t, BF16),
        potential,
        center,
        halfwidth,
    )
    p, f0, f6, s0, s6 = run(
        call(
            first_kernel,
            "first",
            [HB] + [VM] * 6,
            [layer_shape] + [plane] * 4,
            held + operator_scratch + two_copies,
        ),
        field, gx, gy, gc, k_high, k_low, local,
    )
    r0 = passed_along(f6, "face", 1)
    r6 = passed_along(f0, "face", -1)
    q0 = passed_along(s6, "slab", 1)
    q6 = passed_along(s0, "slab", -1)
    r_high, r_low, far_high, far_low = run(
        call(
            rotation_kernel, "rotation", [SM, VM], [((768, 256), BF16)] * 2 + [((256, 256), BF16)] * 2
        ),
        me, rotation,
    )
    e0, e6 = run(call(cross_kernel, "cross", [VM] * 2, [both] * 2), q0, q6)
    d0 = passed_along(e6, "face", 1)
    d6 = passed_along(e0, "face", -1)
    (layers,) = run(
        call(second_kernel, "second", [VM] * 8, [layer_shape], operator_scratch), p, r0, r6, q0, q6, k_high, k_low, local
    )
    v1, v2, push_x, push_y, push_c = run(
        call(
            third_kernel,
            "third",
            [VM] * 3 + [HB] + [VM] * 3,
            [set1, set2, edge, edge, corners],
            held
            + [
                pltpu.VMEM((CXROWS, LANES), F32),
                pltpu.VMEM((CXROWS, LANES), BF16),
                pltpu.VMEM((CXROWS, LANES), BF16),
                pltpu.VMEM((PARTS, YROWS, LANES), F32),
            ]
            + two_copies,
        ),
        layers, d0, d6, field, c_high, c_low, local,
    )
    l2, r2 = left(v2), right(v2)
    push_x, push_y, push_c = fenced("fence_p", push_x, push_y, push_c)
    ry = passed_along(push_y, "face", 1)
    rx = passed_along(push_x, "slab", 1)
    rc = passed_diagonal(push_c, 1)
    (v1,) = run(call(finish_kernel, "finish", [VM] * 4, [set1], flops=1), v1, rx, ry, rc)
    l1, r1 = left(v1), right(v1)


    def relayed(name, from_left, from_right):
        rows = from_left.shape[0] // PARTS
        parts = run(call(relay_kernel, name, [VM] * 2, [rows_of(rows)] * 2), from_left, from_right)
        return left(parts[0]), right(parts[1])

    far2 = relayed("relay2", l2, r2)
    (total2,) = run(call(near_kernel, "near2", [VM] * 5, [wide2]), v2, l2, r2, r_high, r_low)
    far1 = relayed("relay1", l1, r1)
    result_shape = [((OWNED, 256), F32)]

    def far_scratch(lines):
        return [pltpu.VMEM((len(lines) * NZ, 256), F32), pltpu.SemaphoreType.DMA((len(line_runs(lines)),))]

    (result,) = run(
        call(functools.partial(far_kernel, LINES2), "far2", [VM] * 5, result_shape, far_scratch(LINES2), out=HB),
        total2, *far2, far_high, far_low,
    )
    (total1,) = run(call(near_kernel, "near1", [VM] * 5, [wide1]), v1, l1, r1, r_high, r_low)
    (result,) = run(
        call(
            functools.partial(far_kernel, LINES1),
            "last",
            [VM] * 5 + [HB],
            result_shape,
            far_scratch(LINES1),
            out=HB,
            aliases=((5, 0),),
        ),
        total1, *far1, far_high, far_low, result,
    )
    return result.reshape(6, 6, NZ, 256)


def solution(mesh):
    placed = (
        P("slab", "face", None, "band"),
        P(None, "band"),
        P(),
        P("slab", "face", None),
        P(),
        P(),
    )
    return jax.shard_map(
        shards,
        mesh=mesh,
        in_specs=placed,
        out_specs=P("slab", "face", None, "band"),
        check_vma=False,
    )
```

```python
import functools

import jax
import jax.numpy as jnp
import numpy as np
from jax import lax
from jax.experimental import pallas as pl
from jax.experimental.pallas import tpu as pltpu
from jax.sharding import PartitionSpec as P

ORDER = 6
SIDE = ORDER + 1
NZ = 24
LANES = 128
PARTS = 2
ROWS = 56
CELL_ROWS = SIDE * ROWS
KPAD = 400
LAYER = NZ * ROWS
XROWS = 3 * ORDER * ROWS + KPAD
YROWS = LAYER + ROWS
F32 = jnp.float32
BF16 = jnp.bfloat16
LIMIT = 16 * 1024 * 1024
WHOLE = 60 * 1024 * 1024

LINES1 = [(0, y) for y in range(6)] + [(x, 0) for x in range(1, 6)]
LINES2 = [(x, y) for x in range(1, 6) for y in range(1, 6)]
OWNED = 36 * NZ
SET1 = len(LINES1) * NZ
SET2 = len(LINES2) * NZ
EDGE = 6 * NZ
PLANE = 7 * NZ
PLACES = {(x, y): x * 6 + y for x in range(6) for y in range(6)}
PLACES.update({(6, y): 36 + y for y in range(7)})
PLACES.update({(x, 6): 43 + x for x in range(6)})
CORNERS = ((0, 0), (6, 0), (0, 6), (6, 6))
CROWS = 8
CPAD = 64
CLAYER = NZ * CROWS
CXROWS = 3 * ORDER * CROWS + CPAD


def selection(places, rows, padded):
    chosen = np.zeros((padded, SIDE**3), np.float32)
    for (p, q), row in places:
        for r in range(SIDE):
            chosen[r * rows + row, (p * SIDE + q) * SIDE + r] = 1.0
    return chosen


def split(values):
    high = values.astype(BF16)
    return high, (values - high.astype(F32)).astype(BF16)


def dot(a, b):
    return jnp.dot(a, b, preferred_element_type=F32)


def line(index):
    return pl.ds(index * NZ, NZ)


def carry_out(copies):
    for copy in copies:
        copy.start()
    for copy in copies:
        copy.wait()


def lane_blocks(w, held, sems):
    return [
        pltpu.make_async_copy(
            w.at[:, pl.ds(part * LANES, LANES)], held.at[pl.ds(part * OWNED, OWNED)], sems.at[part]
        )
        for part in range(PARTS)
    ]


def pulls_kernel(w, pull_x, pull_y, pull_c, sems):
    copies = []

    def add(first, rows, out, start, part):
        copies.append(
            pltpu.make_async_copy(
                w.at[pl.ds(first, rows), pl.ds(part * LANES, LANES)],
                out.at[pl.ds(start, rows)],
                sems.at[len(copies)],
            )
        )

    for part in range(PARTS):
        add(0, EDGE, pull_x, part * EDGE, part)
        add(0, NZ, pull_c, part * NZ, part)
        for x in range(6):
            add(x * EDGE, NZ, pull_y, part * EDGE + x * NZ, part)
    carry_out(copies)


def cell_kernel(
    cell, chosen, chosen_t, potential, center, halfwidth, k_high, k_low, local, cell_ref, chosen_ref, chosen_t_ref, sems
):
    pairs = ((cell, cell_ref), (chosen, chosen_ref), (chosen_t, chosen_t_ref))
    copies = [pltpu.make_async_copy(source, target, sems.at[index]) for index, (source, target) in enumerate(pairs)]
    for copy in copies:
        copy.start()
    scale = 1.0 / jnp.broadcast_to(halfwidth[...], (1, LANES))
    local[...] = jnp.zeros_like(local)
    for x in range(6):
        shifted = potential[x] - center[...]
        for z in range(NZ):
            local[pl.ds(z * ROWS + x * 6, 6)] = shifted[:, z : z + 1] * scale
    for copy in copies:
        copy.wait()
    for half, k_ref in zip(split(cell_ref[...] * scale[:, 0:1]), (k_high, k_low)):
        k_ref[...] = dot(dot(chosen_ref[...], half).astype(BF16), chosen_t_ref[...]).astype(BF16)


def rotation_kernel(me, rotation, k_high, k_low, columns, r_high, r_low, far_high, far_low, c_high, c_low):
    c_high[...] = dot(k_high[...], columns[...]).astype(BF16)
    c_low[...] = dot(k_low[...], columns[...]).astype(BF16)
    for index, steps in enumerate((0, -1, 1, 2)):
        owner = lax.rem(me[0] + steps + 4, 4)
        high, low = split(rotation[pl.ds(pl.multiple_of(owner * 256, 256), 256)])
        if index < 3:
            r_high[pl.ds(index * 256, 256)] = high
            r_low[pl.ds(index * 256, 256)] = low
        else:
            far_high[...] = high
            far_low[...] = low


def turned(values, r_high, r_low):
    high, low = split(values)
    rh = r_high[...]
    return dot(high, rh) + (dot(low, rh) + dot(high, r_low[...]))


def side_by_side(stacked):
    rows = stacked.shape[0] // PARTS
    return [stacked[pl.ds(part * rows, rows)] for part in range(PARTS)]


def near_kernel(own, left, right, r_high, r_low, total):
    pieces = side_by_side(own) + side_by_side(left) + side_by_side(right)
    total[...] = turned(jnp.concatenate(pieces, 1), r_high, r_low)


def line_runs(lines):
    runs = []
    for index, (x, y) in enumerate(lines):
        there = x * 6 + y
        if runs and runs[-1][0] + runs[-1][2] == there:
            runs[-1][2] += 1
        else:
            runs.append([there, index, 1])
    return runs


def write_lines(lines, held, out, sems):
    carry_out(
        [
            pltpu.make_async_copy(
                held.at[pl.ds(here * NZ, count * NZ)], out.at[pl.ds(there * NZ, count * NZ)], sems.at[index]
            )
            for index, (there, here, count) in enumerate(line_runs(lines))
        ]
    )


def relay_kernel(left, right, left_part, right_part):
    rows = left_part.shape[0]
    left_part[...] = left[0:rows]
    right_part[...] = right[rows:]


def far_kernel(lines, total, far_a, far_b, far_high, far_low, *refs):
    out, held, sems = refs[-3:]
    held[...] = total[...] + turned(jnp.concatenate([far_a[...], far_b[...]], 1), far_high, far_low)
    write_lines(lines, held, out, sems)


def fence_kernel(*refs):
    pass


def cells_product(parts, x_ref, y_ref, xh_ref, xl_ref, k_high, k_low):
    kh = k_high[...]
    kl = k_low[...]
    step = ORDER * ROWS
    for part in range(parts):
        high, low = split(x_ref[part])
        xh_ref[...] = high
        xl_ref[...] = low
        y_ref[part] = jnp.zeros((YROWS, LANES), F32)
        for pair in range(2):
            first, second = 2 * pair * step, (2 * pair + 1) * step
            xh = jnp.concatenate([xh_ref[first : first + KPAD], xh_ref[second : second + KPAD]], 1)
            xl = jnp.concatenate([xl_ref[first : first + KPAD], xl_ref[second : second + KPAD]], 1)
            product = dot(kh, xh) + (dot(kh, xl) + dot(kl, xh))
            y_ref[part, first : first + CELL_ROWS] += product[:CELL_ROWS, :LANES]
            y_ref[part, second : second + CELL_ROWS] += product[:CELL_ROWS, LANES:]
        y_ref[part, 0:ROWS] += y_ref[part, LAYER:YROWS]


def every(start, count):
    return pl.ds(start, count, stride=NZ)


def first_kernel(
    w, gx, gy, gc, k_high, k_low, local, p_out, f0, f6, s0, s6, held, x_ref, y_ref, xh_ref, xl_ref, sems
):
    carry_out(lane_blocks(w, held, sems))
    for part in range(PARTS):
        xs = x_ref.at[part]
        xs[LAYER:] = jnp.zeros((XROWS - LAYER, LANES), F32)
        for z in range(NZ):
            at = z * ROWS
            xs[at : at + 36] = held[every(part * OWNED + z, 36)]
            xs[at + 36 : at + 42] = gx[every(part * EDGE + z, 6)]
            xs[at + 42 : at + 43] = gc[part * NZ + z : part * NZ + z + 1]
            xs[at + 43 : at + 49] = gy[every(part * EDGE + z, 6)]
            xs[at + 49 : at + 56] = jnp.zeros((7, LANES), F32)
        xs[LAYER:YROWS] = xs[0:ROWS]
    cells_product(PARTS, x_ref, y_ref, xh_ref, xl_ref, k_high, k_low)
    for part in range(PARTS):
        ps = p_out.at[part]
        ps[...] = y_ref[part, 0:LAYER] + local[...] * x_ref[part, 0:LAYER]
        base = part * PLANE
        for z in range(NZ):
            at = z * ROWS
            s6[every(base + z, 7)] = ps[at + 36 : at + 43]
            s0[every(base + z, 6)] = ps[at : at + 6]
            s0[base + EDGE + z : base + EDGE + z + 1] = ps[at + 43 : at + 44]
            f0[base + z : base + z + 1] = ps[at : at + 1]
            f0[every(base + NZ + z, 5)] = ps[pl.ds(at + 6, 5, stride=6)]
            f0[base + EDGE + z : base + EDGE + z + 1] = ps[at + 36 : at + 37]
            f6[every(base + z, 6)] = ps[at + 43 : at + 49]
            f6[base + EDGE + z : base + EDGE + z + 1] = ps[at + 42 : at + 43]


def cross_kernel(q0, q6, d0, d6):
    for part in range(PARTS):
        base, there = part * PLANE, part * 2 * NZ
        for index, q in enumerate((q0, q6)):
            d0[pl.ds(there + index * NZ, NZ)] = q[pl.ds(base, NZ)]
            d6[pl.ds(there + index * NZ, NZ)] = q[pl.ds(base + EDGE, NZ)]


def second_kernel(p_in, r0, r6, q0, q6, k_high, k_low, local, layers, x_ref, y_ref, xh_ref, xl_ref):
    for part in range(PARTS):
        xs = x_ref.at[part]
        xs[0:LAYER] = p_in[part]
        xs[LAYER:] = jnp.zeros((XROWS - LAYER, LANES), F32)
        base = part * PLANE
        for z in range(NZ):
            at = z * ROWS
            xs[at : at + 6] += q0[every(base + z, 6)]
            xs[at + 36 : at + 43] += q6[every(base + z, 7)]
            xs[at + 43 : at + 44] += q0[base + EDGE + z : base + EDGE + z + 1]
            xs[at : at + 1] += r0[base + z : base + z + 1]
            xs[pl.ds(at + 6, 5, stride=6)] += r0[every(base + NZ + z, 5)]
            xs[at + 36 : at + 37] += r0[base + EDGE + z : base + EDGE + z + 1]
            xs[at + 43 : at + 49] += r6[every(base + z, 6)]
            xs[at + 42 : at + 43] += r6[base + EDGE + z : base + EDGE + z + 1]
        xs[LAYER:YROWS] = xs[0:ROWS]
    cells_product(PARTS, x_ref, y_ref, xh_ref, xl_ref, k_high, k_low)
    for part in range(PARTS):
        layers[part] = 2.0 * (y_ref[part, 0:LAYER] + local[...] * x_ref[part, 0:LAYER])


def third_kernel(
    layers, d0, d6, w, c_high, c_low, local, set1, set2, push_x, push_y, push_c,
    held, c_ref, ch_ref, cl_ref, y_ref, sems,
):
    copies = lane_blocks(w, held, sems)
    for copy in copies:
        copy.start()
    ch, cl = c_high[...], c_low[...]
    step = ORDER * CROWS
    for part in range(PARTS):
        c_ref[...] = jnp.zeros_like(c_ref)
        base = part * 2 * NZ
        for z in range(NZ):
            at = z * CROWS
            c_ref[at : at + 2] = d0[every(base + z, 2)]
            c_ref[at + 2 : at + 4] = d6[every(base + z, 2)]
        c_ref[CLAYER : CLAYER + CROWS] = c_ref[0:CROWS]
        ch_ref[...], cl_ref[...] = split(2.0 * c_ref[...])
        ys = y_ref.at[part]
        ys[0:LAYER] = layers[part]
        ys[LAYER:YROWS] = jnp.zeros((ROWS, LANES), F32)
        for pair in range(2):
            first, second = 2 * pair, 2 * pair + 1
            high = jnp.concatenate([ch_ref[cell * step : cell * step + CPAD] for cell in (first, second)], 1)
            low = jnp.concatenate([cl_ref[cell * step : cell * step + CPAD] for cell in (first, second)], 1)
            product = dot(ch, high) + (dot(ch, low) + dot(cl, high))
            for index, cell in enumerate((first, second)):
                start = cell * ORDER * ROWS
                ys[start : start + CELL_ROWS] += product[:CELL_ROWS, index * LANES : (index + 1) * LANES]
        ys[0:ROWS] += ys[LAYER:YROWS]
        base1, base2 = part * SET1, part * SET2
        for z in range(NZ):
            at = z * ROWS
            ys[at : at + 1] += 2.0 * (local[at : at + 1] * c_ref[z * CROWS : z * CROWS + 1])
            set1[every(base1 + z, 6)] = ys[at : at + 6]
            set1[every(base1 + EDGE + z, 5)] = ys[pl.ds(at + 6, 5, stride=6)]
            for x in range(1, 6):
                set2[every(base2 + 5 * (x - 1) * NZ + z, 5)] = ys[at + 6 * x + 1 : at + 6 * x + 6]
            push_x[every(part * EDGE + z, 6)] = ys[at + 36 : at + 42]
            push_c[part * NZ + z : part * NZ + z + 1] = ys[at + 42 : at + 43]
            push_y[every(part * EDGE + z, 6)] = ys[at + 43 : at + 49]
    for copy in copies:
        copy.wait()
    for part in range(PARTS):
        for lines, out in ((LINES1, set1), (LINES2, set2)):
            for index, (x, y) in enumerate(lines):
                out[line(part * len(lines) + index)] -= held[line(part * 36 + x * 6 + y)]


def finish_kernel(set1, rx, ry, rc, out):
    out[...] = set1[...]
    for part in range(PARTS):
        base, edge = part * SET1, part * EDGE
        out[pl.ds(base, EDGE)] += rx[pl.ds(edge, EDGE)]
        out[pl.ds(base, NZ)] += ry[pl.ds(edge, NZ)] + rc[pl.ds(part * NZ, NZ)]
        out[pl.ds(base + EDGE, 5 * NZ)] += ry[pl.ds(edge + NZ, 5 * NZ)]


VM = pl.BlockSpec(memory_space=pltpu.VMEM)
HB = pl.BlockSpec(memory_space=pltpu.HBM)
ANYWHERE = pl.BlockSpec(memory_space=pl.ANY)
SM = pl.BlockSpec(memory_space=pltpu.SMEM)


def call(kernel, name, in_specs, shapes, scratch=(), out=None, aliases=(), flops=10**10, limit=LIMIT, ordered=True):
    inputs, outputs = len(in_specs), len(shapes)
    tokens = 1 if ordered else 0

    def body(*refs):
        kernel(*refs[:inputs], *refs[inputs + tokens : inputs + tokens + outputs], *refs[inputs + outputs + 2 * tokens :])

    if out is None:
        results = [pltpu.VMEM(*shape) for shape in shapes]
    else:
        results = [jax.ShapeDtypeStruct(*shape) for shape in shapes]
    return pl.pallas_call(
        body,
        name=name,
        in_specs=in_specs + [ANYWHERE] * tokens,
        out_specs=[out or VM] * outputs + [ANYWHERE] * tokens,
        out_shape=results + [jax.ShapeDtypeStruct((8, LANES), F32)] * tokens,
        scratch_shapes=list(scratch),
        compiler_params=pltpu.CompilerParams(vmem_limit_bytes=limit),
        cost_estimate=pl.CostEstimate(flops=flops, bytes_accessed=1, transcendentals=0),
        input_output_aliases={**({inputs: outputs} if ordered else {}), **dict(aliases)},
    )


class Sequence:
    def __init__(self):
        self.token = jnp.zeros((8, LANES), F32)

    def __call__(self, kernel, *operands):
        *results, self.token = kernel(*operands, self.token)
        return results


def rows_of(count):
    return ((count, LANES), F32)


def passed_along(value, axis, steps):
    count = lax.axis_size(axis)
    return lax.ppermute(value, axis, [(s, (s + steps) % count) for s in range(count)])


def passed_diagonal(value, steps):
    slabs, faces = lax.axis_size("slab"), lax.axis_size("face")
    pairs = [
        (a * faces + b, ((a + steps) % slabs) * faces + (b + steps) % faces)
        for a in range(slabs)
        for b in range(faces)
    ]
    return lax.ppermute(value, ("slab", "face"), pairs)


def shards(wavefunctions, rotation, cell_matrix, potential, center, halfwidth):
    run = Sequence()
    places = PLACES.items()
    chosen = selection(places, ROWS, KPAD)
    columns = chosen @ selection([(place, row) for row, place in enumerate(CORNERS)], CROWS, CPAD).T
    me = lax.axis_index("band").astype(jnp.int32).reshape(1)
    held = [pltpu.VMEM((PARTS * OWNED, LANES), F32)]
    operator_scratch = [
        pltpu.VMEM((PARTS, XROWS, LANES), F32),
        pltpu.VMEM((PARTS, YROWS, LANES), F32),
        pltpu.VMEM((XROWS, LANES), BF16),
        pltpu.VMEM((XROWS, LANES), BF16),
    ]
    two_copies = [pltpu.SemaphoreType.DMA((PARTS,))]
    edge, plane, corners = rows_of(PARTS * EDGE), rows_of(PARTS * PLANE), rows_of(PARTS * NZ)
    both = rows_of(PARTS * 2 * NZ)
    set1, set2 = rows_of(PARTS * SET1), rows_of(PARTS * SET2)
    wide1, wide2 = ((SET1, 256), F32), ((SET2, 256), F32)
    layer_shape = ((PARTS, LAYER, LANES), F32)
    field = wavefunctions.reshape(OWNED, 256)

    def left(value):
        return passed_along(value, "band", 1)

    def right(value):
        return passed_along(value, "band", -1)

    def fenced(name, *values):
        shapes = [(value.shape, value.dtype) for value in values]
        count = len(values)
        aliases = [(index, index) for index in range(count)]
        return run(call(fence_kernel, name, [ANYWHERE] * count, shapes, out=ANYWHERE, aliases=aliases), *values)

    pull_x, pull_y, pull_c = call(
        pulls_kernel,
        "pulls",
        [HB],
        [edge, edge, corners],
        [pltpu.SemaphoreType.DMA((8 * PARTS,))],
        limit=WHOLE,
        ordered=False,
    )(field)
    gy = passed_along(pull_y, "face", -1)
    gx = passed_along(pull_x, "slab", -1)
    (pull_c,) = fenced("fence_c", pull_c)
    gc = passed_diagonal(pull_c, -1)
    k_high, k_low, local = run(
        call(
            cell_kernel,
            "cell",
            [HB] * 3 + [VM] * 3,
            [((KPAD, KPAD), BF16)] * 2 + [((LAYER, LANES), F32)],
            [
                pltpu.VMEM((SIDE**3, SIDE**3), F32),
                pltpu.VMEM((KPAD, SIDE**3), BF16),
                pltpu.VMEM((SIDE**3, KPAD), BF16),
                pltpu.SemaphoreType.DMA((3,)),
            ],
            flops=1,
        ),
        cell_matrix,
        jnp.asarray(chosen, BF16),
        jnp.asarray(chosen.T, BF16),
        potential,
        center.reshape(1, 1),
        halfwidth.reshape(1, 1),
    )
    p, f0, f6, s0, s6 = run(
        call(
            first_kernel,
            "first",
            [HB] + [VM] * 6,
            [layer_shape] + [plane] * 4,
            held + operator_scratch + two_copies,
        ),
        field, gx, gy, gc, k_high, k_low, local,
    )
    r0 = passed_along(f6, "face", 1)
    r6 = passed_along(f0, "face", -1)
    q0 = passed_along(s6, "slab", 1)
    q6 = passed_along(s0, "slab", -1)
    r_high, r_low, far_high, far_low, c_high, c_low = run(
        call(
            rotation_kernel,
            "rotation",
            [SM] + [VM] * 4,
            [((768, 256), BF16)] * 2 + [((256, 256), BF16)] * 2 + [((KPAD, CPAD), BF16)] * 2,
        ),
        me, rotation, k_high, k_low, jnp.asarray(columns, BF16),
    )
    e0, e6 = run(call(cross_kernel, "cross", [VM] * 2, [both] * 2), q0, q6)
    d0 = passed_along(e6, "face", 1)
    d6 = passed_along(e0, "face", -1)
    (layers,) = run(
        call(second_kernel, "second", [VM] * 8, [layer_shape], operator_scratch), p, r0, r6, q0, q6, k_high, k_low, local
    )
    v1, v2, push_x, push_y, push_c = run(
        call(
            third_kernel,
            "third",
            [VM] * 3 + [HB] + [VM] * 3,
            [set1, set2, edge, edge, corners],
            held
            + [
                pltpu.VMEM((CXROWS, LANES), F32),
                pltpu.VMEM((CXROWS, LANES), BF16),
                pltpu.VMEM((CXROWS, LANES), BF16),
                pltpu.VMEM((PARTS, YROWS, LANES), F32),
            ]
            + two_copies,
        ),
        layers, d0, d6, field, c_high, c_low, local,
    )
    l2, r2 = left(v2), right(v2)
    push_x, push_y, push_c = fenced("fence_p", push_x, push_y, push_c)
    ry = passed_along(push_y, "face", 1)
    rx = passed_along(push_x, "slab", 1)
    rc = passed_diagonal(push_c, 1)
    (v1,) = run(call(finish_kernel, "finish", [VM] * 4, [set1], flops=1), v1, rx, ry, rc)
    l1, r1 = left(v1), right(v1)


    def relayed(name, from_left, from_right):
        rows = from_left.shape[0] // PARTS
        parts = run(call(relay_kernel, name, [VM] * 2, [rows_of(rows)] * 2), from_left, from_right)
        return left(parts[0]), right(parts[1])

    far2 = relayed("relay2", l2, r2)
    (total2,) = run(call(near_kernel, "near2", [VM] * 5, [wide2]), v2, l2, r2, r_high, r_low)
    far1 = relayed("relay1", l1, r1)
    result_shape = [((OWNED, 256), F32)]

    def far_scratch(lines):
        return [pltpu.VMEM((len(lines) * NZ, 256), F32), pltpu.SemaphoreType.DMA((len(line_runs(lines)),))]

    (result,) = run(
        call(functools.partial(far_kernel, LINES2), "far2", [VM] * 5, result_shape, far_scratch(LINES2), out=HB),
        total2, *far2, far_high, far_low,
    )
    (total1,) = run(call(near_kernel, "near1", [VM] * 5, [wide1]), v1, l1, r1, r_high, r_low)
    (result,) = run(
        call(
            functools.partial(far_kernel, LINES1),
            "last",
            [VM] * 5 + [HB],
            result_shape,
            far_scratch(LINES1),
            out=HB,
            aliases=((5, 0),),
        ),
        total1, *far1, far_high, far_low, result,
    )
    return result.reshape(6, 6, NZ, 256)


def solution(mesh):
    placed = (
        P("slab", "face", None, "band"),
        P(None, "band"),
        P(),
        P("slab", "face", None),
        P(),
        P(),
    )
    return jax.shard_map(
        shards,
        mesh=mesh,
        in_specs=placed,
        out_specs=P("slab", "face", None, "band"),
        check_vma=False,
    )
```

```python
import functools

import jax
import jax.numpy as jnp
import numpy as np
from jax import lax
from jax.experimental import pallas as pl
from jax.experimental.pallas import tpu as pltpu
from jax.sharding import PartitionSpec as P

ORDER = 6
SIDE = ORDER + 1
NZ = 24
LANES = 128
PARTS = 2
ROWS = 56
CELL_ROWS = SIDE * ROWS
KPAD = 400
LAYER = NZ * ROWS
XROWS = 3 * ORDER * ROWS + KPAD
YROWS = LAYER + ROWS
F32 = jnp.float32
BF16 = jnp.bfloat16
LIMIT = 16 * 1024 * 1024
WHOLE = 60 * 1024 * 1024

LINES1 = [(0, y) for y in range(6)] + [(x, 0) for x in range(1, 6)]
LINES2 = [(x, y) for x in range(1, 6) for y in range(1, 6)]
OWNED = 36 * NZ
SET1 = len(LINES1) * NZ
SET2 = len(LINES2) * NZ
EDGE = 6 * NZ
PLANE = 7 * NZ
PLACES = {(x, y): x * 6 + y for x in range(6) for y in range(6)}
PLACES.update({(6, y): 36 + y for y in range(7)})
PLACES.update({(x, 6): 43 + x for x in range(6)})
CORNERS = ((0, 0), (6, 0), (0, 6), (6, 6))
CROWS = 8
CPAD = 64
CLAYER = NZ * CROWS
CXROWS = 3 * ORDER * CROWS + CPAD


def selection(places, rows, padded):
    chosen = np.zeros((padded, SIDE**3), np.float32)
    for (p, q), row in places:
        for r in range(SIDE):
            chosen[r * rows + row, (p * SIDE + q) * SIDE + r] = 1.0
    return chosen


def split(values):
    high = values.astype(BF16)
    return high, (values - high.astype(F32)).astype(BF16)


def dot(a, b):
    return jnp.dot(a, b, preferred_element_type=F32)


def line(index):
    return pl.ds(index * NZ, NZ)


def carry_out(copies):
    for copy in copies:
        copy.start()
    for copy in copies:
        copy.wait()


def lane_blocks(w, held, sems):
    return [
        pltpu.make_async_copy(
            w.at[:, pl.ds(part * LANES, LANES)], held.at[pl.ds(part * OWNED, OWNED)], sems.at[part]
        )
        for part in range(PARTS)
    ]


def pulls_kernel(w, pull_x, pull_y, pull_c, sems):
    copies = []

    def add(first, rows, out, start, part):
        copies.append(
            pltpu.make_async_copy(
                w.at[pl.ds(first, rows), pl.ds(part * LANES, LANES)],
                out.at[pl.ds(start, rows)],
                sems.at[len(copies)],
            )
        )

    for part in range(PARTS):
        add(0, EDGE, pull_x, part * EDGE, part)
        add(0, NZ, pull_c, part * NZ, part)
        for x in range(6):
            add(x * EDGE, NZ, pull_y, part * EDGE + x * NZ, part)
    carry_out(copies)


def cell_kernel(
    cell, chosen, chosen_t, potential, center, halfwidth, k_high, k_low, local, cell_ref, chosen_ref, chosen_t_ref, sems
):
    pairs = ((cell, cell_ref), (chosen, chosen_ref), (chosen_t, chosen_t_ref))
    copies = [pltpu.make_async_copy(source, target, sems.at[index]) for index, (source, target) in enumerate(pairs)]
    for copy in copies:
        copy.start()
    scale = 1.0 / jnp.broadcast_to(halfwidth[...], (1, LANES))
    local[...] = jnp.zeros_like(local)
    for x in range(6):
        shifted = potential[x] - center[...]
        for z in range(NZ):
            local[pl.ds(z * ROWS + x * 6, 6)] = shifted[:, z : z + 1] * scale
    for copy in copies:
        copy.wait()
    for half, k_ref in zip(split(cell_ref[...] * scale[:, 0:1]), (k_high, k_low)):
        k_ref[...] = dot(dot(chosen_ref[...], half).astype(BF16), chosen_t_ref[...]).astype(BF16)


def rotation_kernel(me, rotation, k_high, k_low, columns_high, columns_low, r_high, r_low, far_high, far_low, c_terms):
    c_terms[...] = (dot(k_high[...], columns_high[...]) + dot(k_low[...], columns_low[...])).astype(BF16)
    for index, steps in enumerate((0, -1, 1, 2)):
        owner = lax.rem(me[0] + steps + 4, 4)
        high, low = split(rotation[pl.ds(pl.multiple_of(owner * 256, 256), 256)])
        if index < 3:
            r_high[pl.ds(index * 256, 256)] = high
            r_low[pl.ds(index * 256, 256)] = low
        else:
            far_high[...] = high
            far_low[...] = low


def turned(values, r_high, r_low):
    high, low = split(values)
    rh = r_high[...]
    return dot(high, rh) + (dot(low, rh) + dot(high, r_low[...]))


def side_by_side(stacked):
    rows = stacked.shape[0] // PARTS
    return [stacked[pl.ds(part * rows, rows)] for part in range(PARTS)]


def near_kernel(own, left, right, r_high, r_low, total):
    pieces = side_by_side(own) + side_by_side(left) + side_by_side(right)
    total[...] = turned(jnp.concatenate(pieces, 1), r_high, r_low)


def line_runs(lines):
    runs = []
    for index, (x, y) in enumerate(lines):
        there = x * 6 + y
        if runs and runs[-1][0] + runs[-1][2] == there:
            runs[-1][2] += 1
        else:
            runs.append([there, index, 1])
    return runs


def write_lines(lines, held, out, sems):
    carry_out(
        [
            pltpu.make_async_copy(
                held.at[pl.ds(here * NZ, count * NZ)], out.at[pl.ds(there * NZ, count * NZ)], sems.at[index]
            )
            for index, (there, here, count) in enumerate(line_runs(lines))
        ]
    )


def relay_kernel(left, right, left_part, right_part):
    rows = left_part.shape[0]
    left_part[...] = left[0:rows]
    right_part[...] = right[rows:]


def far_kernel(lines, total, far_a, far_b, far_high, far_low, *refs):
    out, held, sems = refs[-3:]
    held[...] = total[...] + turned(jnp.concatenate([far_a[...], far_b[...]], 1), far_high, far_low)
    write_lines(lines, held, out, sems)


def fence_kernel(*refs):
    pass


def cells_product(parts, x_ref, y_ref, xh_ref, xl_ref, k_high, k_low):
    kh = k_high[...]
    kl = k_low[...]
    step = ORDER * ROWS
    for part in range(parts):
        high, low = split(x_ref[part])
        xh_ref[...] = high
        xl_ref[...] = low
        y_ref[part] = jnp.zeros((YROWS, LANES), F32)
        for pair in range(2):
            first, second = 2 * pair * step, (2 * pair + 1) * step
            xh = jnp.concatenate([xh_ref[first : first + KPAD], xh_ref[second : second + KPAD]], 1)
            xl = jnp.concatenate([xl_ref[first : first + KPAD], xl_ref[second : second + KPAD]], 1)
            product = dot(kh, xh) + (dot(kh, xl) + dot(kl, xh))
            y_ref[part, first : first + CELL_ROWS] += product[:CELL_ROWS, :LANES]
            y_ref[part, second : second + CELL_ROWS] += product[:CELL_ROWS, LANES:]
        y_ref[part, 0:ROWS] += y_ref[part, LAYER:YROWS]


def every(start, count):
    return pl.ds(start, count, stride=NZ)


def first_kernel(
    w, gx, gy, gc, k_high, k_low, local, p_out, f0, f6, s0, s6, held, x_ref, y_ref, xh_ref, xl_ref, sems
):
    carry_out(lane_blocks(w, held, sems))
    for part in range(PARTS):
        xs = x_ref.at[part]
        xs[LAYER:] = jnp.zeros((XROWS - LAYER, LANES), F32)
        for z in range(NZ):
            at = z * ROWS
            xs[at : at + 36] = held[every(part * OWNED + z, 36)]
            xs[at + 36 : at + 42] = gx[every(part * EDGE + z, 6)]
            xs[at + 42 : at + 43] = gc[part * NZ + z : part * NZ + z + 1]
            xs[at + 43 : at + 49] = gy[every(part * EDGE + z, 6)]
            xs[at + 49 : at + 56] = jnp.zeros((7, LANES), F32)
        xs[LAYER:YROWS] = xs[0:ROWS]
    cells_product(PARTS, x_ref, y_ref, xh_ref, xl_ref, k_high, k_low)
    for part in range(PARTS):
        ps = p_out.at[part]
        ps[...] = y_ref[part, 0:LAYER] + local[...] * x_ref[part, 0:LAYER]
        base = part * PLANE
        for z in range(NZ):
            at = z * ROWS
            s6[every(base + z, 7)] = ps[at + 36 : at + 43]
            s0[every(base + z, 6)] = ps[at : at + 6]
            s0[base + EDGE + z : base + EDGE + z + 1] = ps[at + 43 : at + 44]
            f0[base + z : base + z + 1] = ps[at : at + 1]
            f0[every(base + NZ + z, 5)] = ps[pl.ds(at + 6, 5, stride=6)]
            f0[base + EDGE + z : base + EDGE + z + 1] = ps[at + 36 : at + 37]
            f6[every(base + z, 6)] = ps[at + 43 : at + 49]
            f6[base + EDGE + z : base + EDGE + z + 1] = ps[at + 42 : at + 43]


def cross_kernel(q0, q6, d0, d6):
    for part in range(PARTS):
        base, there = part * PLANE, part * 2 * NZ
        for index, q in enumerate((q0, q6)):
            d0[pl.ds(there + index * NZ, NZ)] = q[pl.ds(base, NZ)]
            d6[pl.ds(there + index * NZ, NZ)] = q[pl.ds(base + EDGE, NZ)]


def second_kernel(p_in, r0, r6, q0, q6, k_high, k_low, local, layers, x_ref, y_ref, xh_ref, xl_ref):
    for part in range(PARTS):
        xs = x_ref.at[part]
        xs[0:LAYER] = p_in[part]
        xs[LAYER:] = jnp.zeros((XROWS - LAYER, LANES), F32)
        base = part * PLANE
        for z in range(NZ):
            at = z * ROWS
            xs[at : at + 6] += q0[every(base + z, 6)]
            xs[at + 36 : at + 43] += q6[every(base + z, 7)]
            xs[at + 43 : at + 44] += q0[base + EDGE + z : base + EDGE + z + 1]
            xs[at : at + 1] += r0[base + z : base + z + 1]
            xs[pl.ds(at + 6, 5, stride=6)] += r0[every(base + NZ + z, 5)]
            xs[at + 36 : at + 37] += r0[base + EDGE + z : base + EDGE + z + 1]
            xs[at + 43 : at + 49] += r6[every(base + z, 6)]
            xs[at + 42 : at + 43] += r6[base + EDGE + z : base + EDGE + z + 1]
        xs[LAYER:YROWS] = xs[0:ROWS]
    cells_product(PARTS, x_ref, y_ref, xh_ref, xl_ref, k_high, k_low)
    for part in range(PARTS):
        layers[part] = 2.0 * (y_ref[part, 0:LAYER] + local[...] * x_ref[part, 0:LAYER])


def third_kernel(
    layers, d0, d6, w, c_terms, local, set1, set2, push_x, push_y, push_c,
    held, c_ref, ch_ref, cl_ref, y_ref, sems,
):
    copies = lane_blocks(w, held, sems)
    for copy in copies:
        copy.start()
    terms = c_terms[...]
    step = ORDER * CROWS
    for part in range(PARTS):
        c_ref[...] = jnp.zeros_like(c_ref)
        base = part * 2 * NZ
        for z in range(NZ):
            at = z * CROWS
            c_ref[at : at + 2] = d0[every(base + z, 2)]
            c_ref[at + 2 : at + 4] = d6[every(base + z, 2)]
        c_ref[CLAYER : CLAYER + CROWS] = c_ref[0:CROWS]
        ch_ref[...], cl_ref[...] = split(2.0 * c_ref[...])
        ys = y_ref.at[part]
        ys[0:LAYER] = layers[part]
        ys[LAYER:YROWS] = jnp.zeros((ROWS, LANES), F32)
        for pair in range(2):
            first, second = 2 * pair, 2 * pair + 1
            high = jnp.concatenate([ch_ref[cell * step : cell * step + CPAD] for cell in (first, second)], 1)
            low = jnp.concatenate([cl_ref[cell * step : cell * step + CPAD] for cell in (first, second)], 1)
            product = dot(terms, jnp.concatenate([high, low, high], 0))
            for index, cell in enumerate((first, second)):
                start = cell * ORDER * ROWS
                ys[start : start + CELL_ROWS] += product[:CELL_ROWS, index * LANES : (index + 1) * LANES]
        ys[0:ROWS] += ys[LAYER:YROWS]
        base1, base2 = part * SET1, part * SET2
        for z in range(NZ):
            at = z * ROWS
            ys[at : at + 1] += 2.0 * (local[at : at + 1] * c_ref[z * CROWS : z * CROWS + 1])
            set1[every(base1 + z, 6)] = ys[at : at + 6]
            set1[every(base1 + EDGE + z, 5)] = ys[pl.ds(at + 6, 5, stride=6)]
            for x in range(1, 6):
                set2[every(base2 + 5 * (x - 1) * NZ + z, 5)] = ys[at + 6 * x + 1 : at + 6 * x + 6]
            push_x[every(part * EDGE + z, 6)] = ys[at + 36 : at + 42]
            push_c[part * NZ + z : part * NZ + z + 1] = ys[at + 42 : at + 43]
            push_y[every(part * EDGE + z, 6)] = ys[at + 43 : at + 49]
    for copy in copies:
        copy.wait()
    for part in range(PARTS):
        for lines, out in ((LINES1, set1), (LINES2, set2)):
            for index, (x, y) in enumerate(lines):
                out[line(part * len(lines) + index)] -= held[line(part * 36 + x * 6 + y)]


def finish_kernel(set1, rx, ry, rc, out):
    out[...] = set1[...]
    for part in range(PARTS):
        base, edge = part * SET1, part * EDGE
        out[pl.ds(base, EDGE)] += rx[pl.ds(edge, EDGE)]
        out[pl.ds(base, NZ)] += ry[pl.ds(edge, NZ)] + rc[pl.ds(part * NZ, NZ)]
        out[pl.ds(base + EDGE, 5 * NZ)] += ry[pl.ds(edge + NZ, 5 * NZ)]


VM = pl.BlockSpec(memory_space=pltpu.VMEM)
HB = pl.BlockSpec(memory_space=pltpu.HBM)
ANYWHERE = pl.BlockSpec(memory_space=pl.ANY)
SM = pl.BlockSpec(memory_space=pltpu.SMEM)


def call(kernel, name, in_specs, shapes, scratch=(), out=None, aliases=(), flops=10**10, limit=LIMIT, ordered=True):
    inputs, outputs = len(in_specs), len(shapes)
    tokens = 1 if ordered else 0

    def body(*refs):
        kernel(*refs[:inputs], *refs[inputs + tokens : inputs + tokens + outputs], *refs[inputs + outputs + 2 * tokens :])

    if out is None:
        results = [pltpu.VMEM(*shape) for shape in shapes]
    else:
        results = [jax.ShapeDtypeStruct(*shape) for shape in shapes]
    return pl.pallas_call(
        body,
        name=name,
        in_specs=in_specs + [ANYWHERE] * tokens,
        out_specs=[out or VM] * outputs + [ANYWHERE] * tokens,
        out_shape=results + [jax.ShapeDtypeStruct((8, LANES), F32)] * tokens,
        scratch_shapes=list(scratch),
        compiler_params=pltpu.CompilerParams(vmem_limit_bytes=limit),
        cost_estimate=pl.CostEstimate(flops=flops, bytes_accessed=1, transcendentals=0),
        input_output_aliases={**({inputs: outputs} if ordered else {}), **dict(aliases)},
    )


class Sequence:
    def __init__(self):
        self.token = jnp.zeros((8, LANES), F32)

    def __call__(self, kernel, *operands):
        *results, self.token = kernel(*operands, self.token)
        return results


def rows_of(count):
    return ((count, LANES), F32)


def passed_along(value, axis, steps):
    count = lax.axis_size(axis)
    return lax.ppermute(value, axis, [(s, (s + steps) % count) for s in range(count)])


def passed_diagonal(value, steps):
    slabs, faces = lax.axis_size("slab"), lax.axis_size("face")
    pairs = [
        (a * faces + b, ((a + steps) % slabs) * faces + (b + steps) % faces)
        for a in range(slabs)
        for b in range(faces)
    ]
    return lax.ppermute(value, ("slab", "face"), pairs)


def shards(wavefunctions, rotation, cell_matrix, potential, center, halfwidth):
    run = Sequence()
    places = PLACES.items()
    chosen = selection(places, ROWS, KPAD)
    columns = chosen @ selection([(place, row) for row, place in enumerate(CORNERS)], CROWS, CPAD).T
    columns_high = np.concatenate([columns, columns, 0 * columns], 1)
    columns_low = np.concatenate([0 * columns, 0 * columns, columns], 1)
    me = lax.axis_index("band").astype(jnp.int32).reshape(1)
    held = [pltpu.VMEM((PARTS * OWNED, LANES), F32)]
    operator_scratch = [
        pltpu.VMEM((PARTS, XROWS, LANES), F32),
        pltpu.VMEM((PARTS, YROWS, LANES), F32),
        pltpu.VMEM((XROWS, LANES), BF16),
        pltpu.VMEM((XROWS, LANES), BF16),
    ]
    two_copies = [pltpu.SemaphoreType.DMA((PARTS,))]
    edge, plane, corners = rows_of(PARTS * EDGE), rows_of(PARTS * PLANE), rows_of(PARTS * NZ)
    both = rows_of(PARTS * 2 * NZ)
    set1, set2 = rows_of(PARTS * SET1), rows_of(PARTS * SET2)
    wide1, wide2 = ((SET1, 256), F32), ((SET2, 256), F32)
    layer_shape = ((PARTS, LAYER, LANES), F32)
    field = wavefunctions.reshape(OWNED, 256)

    def left(value):
        return passed_along(value, "band", 1)

    def right(value):
        return passed_along(value, "band", -1)

    def fenced(name, *values):
        shapes = [(value.shape, value.dtype) for value in values]
        count = len(values)
        aliases = [(index, index) for index in range(count)]
        return run(call(fence_kernel, name, [ANYWHERE] * count, shapes, out=ANYWHERE, aliases=aliases), *values)

    pull_x, pull_y, pull_c = call(
        pulls_kernel,
        "pulls",
        [HB],
        [edge, edge, corners],
        [pltpu.SemaphoreType.DMA((8 * PARTS,))],
        limit=WHOLE,
        ordered=False,
    )(field)
    gy = passed_along(pull_y, "face", -1)
    gx = passed_along(pull_x, "slab", -1)
    (pull_c,) = fenced("fence_c", pull_c)
    gc = passed_diagonal(pull_c, -1)
    k_high, k_low, local = run(
        call(
            cell_kernel,
            "cell",
            [HB] * 3 + [VM] * 3,
            [((KPAD, KPAD), BF16)] * 2 + [((LAYER, LANES), F32)],
            [
                pltpu.VMEM((SIDE**3, SIDE**3), F32),
                pltpu.VMEM((KPAD, SIDE**3), BF16),
                pltpu.VMEM((SIDE**3, KPAD), BF16),
                pltpu.SemaphoreType.DMA((3,)),
            ],
            flops=1,
        ),
        cell_matrix,
        jnp.asarray(chosen, BF16),
        jnp.asarray(chosen.T, BF16),
        potential,
        center.reshape(1, 1),
        halfwidth.reshape(1, 1),
    )
    p, f0, f6, s0, s6 = run(
        call(
            first_kernel,
            "first",
            [HB] + [VM] * 6,
            [layer_shape] + [plane] * 4,
            held + operator_scratch + two_copies,
        ),
        field, gx, gy, gc, k_high, k_low, local,
    )
    r0 = passed_along(f6, "face", 1)
    r6 = passed_along(f0, "face", -1)
    q0 = passed_along(s6, "slab", 1)
    q6 = passed_along(s0, "slab", -1)
    r_high, r_low, far_high, far_low, c_terms = run(
        call(
            rotation_kernel,
            "rotation",
            [SM] + [VM] * 5,
            [((768, 256), BF16)] * 2 + [((256, 256), BF16)] * 2 + [((KPAD, 3 * CPAD), BF16)],
        ),
        me, rotation, k_high, k_low, jnp.asarray(columns_high, BF16), jnp.asarray(columns_low, BF16),
    )
    e0, e6 = run(call(cross_kernel, "cross", [VM] * 2, [both] * 2), q0, q6)
    d0 = passed_along(e6, "face", 1)
    d6 = passed_along(e0, "face", -1)
    (layers,) = run(
        call(second_kernel, "second", [VM] * 8, [layer_shape], operator_scratch), p, r0, r6, q0, q6, k_high, k_low, local
    )
    v1, v2, push_x, push_y, push_c = run(
        call(
            third_kernel,
            "third",
            [VM] * 3 + [HB] + [VM] * 2,
            [set1, set2, edge, edge, corners],
            held
            + [
                pltpu.VMEM((CXROWS, LANES), F32),
                pltpu.VMEM((CXROWS, LANES), BF16),
                pltpu.VMEM((CXROWS, LANES), BF16),
                pltpu.VMEM((PARTS, YROWS, LANES), F32),
            ]
            + two_copies,
        ),
        layers, d0, d6, field, c_terms, local,
    )
    l2, r2 = left(v2), right(v2)
    push_x, push_y, push_c = fenced("fence_p", push_x, push_y, push_c)
    ry = passed_along(push_y, "face", 1)
    rx = passed_along(push_x, "slab", 1)
    rc = passed_diagonal(push_c, 1)
    (v1,) = run(call(finish_kernel, "finish", [VM] * 4, [set1], flops=1), v1, rx, ry, rc)
    l1, r1 = left(v1), right(v1)


    def relayed(name, from_left, from_right):
        rows = from_left.shape[0] // PARTS
        parts = run(call(relay_kernel, name, [VM] * 2, [rows_of(rows)] * 2), from_left, from_right)
        return left(parts[0]), right(parts[1])

    far2 = relayed("relay2", l2, r2)
    (total2,) = run(call(near_kernel, "near2", [VM] * 5, [wide2]), v2, l2, r2, r_high, r_low)
    far1 = relayed("relay1", l1, r1)
    result_shape = [((OWNED, 256), F32)]

    def far_scratch(lines):
        return [pltpu.VMEM((len(lines) * NZ, 256), F32), pltpu.SemaphoreType.DMA((len(line_runs(lines)),))]

    (result,) = run(
        call(functools.partial(far_kernel, LINES2), "far2", [VM] * 5, result_shape, far_scratch(LINES2), out=HB),
        total2, *far2, far_high, far_low,
    )
    (total1,) = run(call(near_kernel, "near1", [VM] * 5, [wide1]), v1, l1, r1, r_high, r_low)
    (result,) = run(
        call(
            functools.partial(far_kernel, LINES1),
            "last",
            [VM] * 5 + [HB],
            result_shape,
            far_scratch(LINES1),
            out=HB,
            aliases=((5, 0),),
        ),
        total1, *far1, far_high, far_low, result,
    )
    return result.reshape(6, 6, NZ, 256)


def solution(mesh):
    placed = (
        P("slab", "face", None, "band"),
        P(None, "band"),
        P(),
        P("slab", "face", None),
        P(),
        P(),
    )
    return jax.shard_map(
        shards,
        mesh=mesh,
        in_specs=placed,
        out_specs=P("slab", "face", None, "band"),
        check_vma=False,
    )
```
